512 devices in a mesh: prov: 32 (over z_lo, y), month: 2 (over core), bin: 8 (over x, z_hi).
Axes of the slice: x: 4, y: 8, z: 8 (z_hi: 2, z_lo: 4; z = z_hi * 4 + z_lo), core: 2. Of those that a mesh axis runs over, the one named last changes fastest.
Arguments:
- tile_values: bfloat16 [4096, 128, 16, 128], P(('prov', 'month', 'bin')), may hold values from -6 to 6
- prov_block: int32 [4096], P(('prov', 'month', 'bin')), may hold values from 0 to 15
- month_block: int32 [4096], P(('prov', 'month', 'bin')), may hold values from 0 to 7
- factor_b: bfloat16 [256, 64], P(('prov', 'month')), may hold values from -0.375 to 0.375
- factor_c: bfloat16 [1024, 64], P(('prov', 'bin')), may hold values from -0.1875 to 0.1875
Outputs:
- factor_a: float32 [65536, 64], P(('prov', 'month', 'bin'))
- new_c: float32 [1024, 64], P(('bin', 'prov', 'month'))
The draws below stay inside these ranges and needn't reach their ends.
All inputs are finite; a program needn't handle non-finite values.
Results may differ from the reference program's by a relative error of at most 0.00053.
Values may be sent and summed in bfloat16 or wider, within the bound.
No kernel may reach another device: no remote copies, remote signals or barrier semaphores. Data moves between devices by JAX's collectives and lax.ppermute only.
A program may use at most 64 MiB of HBM per device.

```python
import math
import jax
import jax.numpy as jnp
import numpy as np
from jax import lax

R = 64
TI = 128
TJ = 16
TK = 128
MB_DEV = 8
PB_DEV = 16
TILES_DEV = 8
PROVIDERS = 65536
MONTHS = 256
BINS = 1024
TILES = 4096
N_MONTH = 2
N_BIN = 8


def with_ends(drawn, own_key, smallest, largest):
    spot = [jax.random.randint(jax.random.fold_in(own_key, axis), (), 0, length) for axis, length in enumerate(drawn.shape)]
    main_axis = drawn.shape.index(max(drawn.shape))
    neighbour = spot[:main_axis] + [(spot[main_axis] + 1) % drawn.shape[main_axis]] + spot[main_axis + 1:]
    return drawn.at[tuple(spot)].set(smallest).at[tuple(neighbour)].set(largest)


def shard_levels(stream_key, extent, cuts, least, largest):
    def one(dim, parts):
        heights = jax.random.uniform(jax.random.fold_in(jax.random.fold_in(stream_key, 6), dim), (parts,), jnp.float32, least / len(cuts), largest / len(cuts))
        return jnp.repeat(jnp.exp(heights), extent[dim] // parts).reshape((-1,) + (1,) * (len(extent) - dim - 1))

    factor_of = one(*cuts[0])
    for cut in cuts[1:]:
        factor_of = factor_of * one(*cut)
    return factor_of


def rank_table(count, skew):
    portions = [(1 << 20) // math.isqrt(standing ** skew) + 1 for standing in range(1, count + 1)]
    scale = 1 + sum(portions) // (1 << 30)
    return np.cumsum(np.array([max(1, weight // scale) for weight in portions]))


def ranked(rng, shape, count, skew):
    table = rank_table(count, skew)
    ticket = jax.random.randint(jax.random.fold_in(rng, 1), shape, 0, int(table[count - 1]))
    grade = jnp.searchsorted(jnp.asarray(table, jnp.int32), ticket, side="right")
    return jax.random.permutation(jax.random.fold_in(rng, 2), count)[grade].astype(jnp.int32)


def noise(key, shape, width, limit, shards=(), kind=jnp.bfloat16):
    gain = shard_levels(key, shape, shards, -0.22, 0.18) if shards else 1.0
    result = jax.random.normal(key, shape, jnp.float32) * width * gain
    return jnp.minimum(jnp.maximum(result, -limit), limit).astype(kind)


def setup_inputs(seed: int = 0) -> dict:
    arg_keys = jax.random.split(jax.random.key(seed), 6)
    return {
        "tile_values": noise(arg_keys[0], (TILES, TI, TJ, TK), 1.0, 6.0, ((0, 512),)),
        "prov_block": with_ends(ranked(arg_keys[1], (TILES,), PB_DEV, 2), jax.random.fold_in(arg_keys[1], 3), 0, PB_DEV - 1).astype(jnp.int32),
        "month_block": with_ends(jax.random.randint(arg_keys[2], (TILES,), 0, MB_DEV), jax.random.fold_in(arg_keys[2], 1), 0, MB_DEV - 1).astype(jnp.int32),
        "factor_b": noise(arg_keys[3], (MONTHS, R), MONTHS ** -0.5, 0.375, ((0, 64),)),
        "factor_c": noise(arg_keys[4], (BINS, R), BINS ** -0.5, 0.1875, ((0, 256),)),
    }


epsilon = 1e-06

def gram_of(factor_rows):
    return jnp.dot(factor_rows.T.astype(jnp.float32), factor_rows.astype(jnp.float32), precision=lax.Precision.HIGHEST, preferred_element_type=jnp.float32)

def solve_gram(gram_matrix, right_rows):
    lower_factor = lax.linalg.cholesky(gram_matrix)
    half_solved = lax.linalg.triangular_solve(lower_factor, right_rows, left_side=False, lower=True, transpose_a=True)
    return lax.linalg.triangular_solve(lower_factor, half_solved, left_side=False, lower=True, transpose_a=False)

def reference(tile_values, prov_block, month_block, factor_b, factor_c):
    factor_rank = factor_b.shape[1]
    tile_owner = jnp.arange(TILES, dtype=jnp.int32) // TILES_DEV
    prov_owner = tile_owner // (N_MONTH * N_BIN)
    month_owner = tile_owner // N_BIN % N_MONTH
    bin_owner = (tile_owner % N_BIN).astype(jnp.int32)
    global_p = (prov_owner * PB_DEV + prov_block).astype(jnp.int32)
    global_m = (month_owner * MB_DEV + month_block).astype(jnp.int32)
    float_b = factor_b.astype(jnp.float32)
    float_c = factor_c.astype(jnp.float32)
    blocks_b = float_b.reshape(MONTHS // TJ, TJ, factor_rank)
    blocks_c = factor_c.reshape(BINS // TK, TK, factor_rank)

    def mode_first(tile_entry):
        tile_block, month_at, bin_at = tile_entry
        product = jnp.dot(tile_block.reshape(TI * TJ, TK).astype(jnp.float32), blocks_c[bin_at].astype(jnp.float32), preferred_element_type=jnp.float32)
        product = product.reshape(TI, TJ, factor_rank)
        return lax.optimization_barrier(jnp.sum(product * blocks_b[month_at][None], axis=1))
    contrib = lax.map(mode_first, (tile_values, global_m, bin_owner))
    mttkrp_a = jax.ops.segment_sum(contrib, global_p, num_segments=PROVIDERS // TI).reshape(PROVIDERS, factor_rank)
    gram_b = gram_of(float_b)
    gram_c = gram_of(float_c)
    factor_a = solve_gram(gram_b * gram_c, mttkrp_a)
    col_scale = jnp.sqrt(lax.optimization_barrier(jnp.sum(factor_a * factor_a, axis=0)) + epsilon)
    hat_a = factor_a / col_scale
    gram_a = gram_of(hat_a)
    blocks_a = hat_a.astype(jnp.bfloat16).reshape(PROVIDERS // TI, TI, factor_rank)

    def mode_last(tile_entry):
        tile_block, prov_at, month_at = tile_entry
        product = jnp.dot(tile_block.reshape(TI, TJ * TK).T.astype(jnp.float32), blocks_a[prov_at].astype(jnp.float32), preferred_element_type=jnp.float32)
        product = product.reshape(TJ, TK, factor_rank)
        return lax.optimization_barrier(jnp.sum(product * blocks_b[month_at][:, None, :], axis=0))
    contrib_c = lax.map(mode_last, (tile_values, global_p, global_m))
    mttkrp_c = jax.ops.segment_sum(contrib_c, bin_owner, num_segments=N_BIN).reshape(BINS, factor_rank)
    new_c = solve_gram(gram_a * gram_b, mttkrp_c)
    return (factor_a, new_c)
```

```python
import jax
import jax.numpy as jnp
from jax import lax
from jax.sharding import PartitionSpec as P

MB_DEV = 8
PB_DEV = 16
epsilon = 1e-06
HIGH = lax.Precision.HIGHEST


def dot32(a, b, dims):
    return lax.dot_general(a, b, (dims, ((), ())), precision=HIGH, preferred_element_type=jnp.float32)


def inverse_factor(gram_matrix):
    lower = lax.linalg.cholesky(gram_matrix)
    eye = jnp.eye(gram_matrix.shape[0], dtype=jnp.float32)
    return lax.linalg.triangular_solve(lower, eye, left_side=True, lower=True)


def apply_inverse(rows, inv_factor):
    half = dot32(rows, inv_factor, ((1,), (1,)))
    return dot32(half, inv_factor, ((1,), (0,)))


def shards(tile_values, prov_block, month_block, factor_b, factor_c):
    tiles, tile_i, tile_j, tile_k = tile_values.shape
    rank = factor_b.shape[1]
    n_prov = lax.axis_size("prov")
    n_month = lax.axis_size("month")
    n_bin = lax.axis_size("bin")
    month = lax.axis_index("month")
    bin_at = lax.axis_index("bin")

    n_all = n_prov * n_month * n_bin
    c_rows = factor_c.shape[0] // n_month
    b_rep = n_bin // factor_b.shape[0]
    own_c_rows = lax.dynamic_slice_in_dim(factor_c, month * c_rows, c_rows, 0).reshape(1, c_rows * rank)
    own_b_row = lax.dynamic_slice_in_dim(factor_b, bin_at // b_rep, 1, 0)
    own_b_row = jnp.concatenate([own_b_row] * c_rows, axis=1)
    chunk = jnp.concatenate([own_c_rows, own_b_row], axis=0)
    sent = jnp.broadcast_to(chunk[None], (n_all,) + chunk.shape)
    got = lax.all_to_all(sent, ("prov", "bin", "month"), 0, 0, tiled=True)
    pairs_c = got[:, 0, :]
    whole_c = pairs_c.reshape(n_all * c_rows, rank)
    whole_b = got[:, 1, :rank].reshape(n_prov, factor_b.shape[0], b_rep, n_month, rank)[:, :, 0]
    whole_b = whole_b.transpose(0, 2, 1, 3).reshape(-1, rank)

    slab_c = lax.dynamic_slice_in_dim(whole_c, bin_at * tile_k, tile_k, 0)
    slab_b = lax.dynamic_slice_in_dim(whole_b, month * (MB_DEV * tile_j), MB_DEV * tile_j, 0)
    slab_b = slab_b.astype(jnp.float32).reshape(MB_DEV, tile_j, rank)
    picked_b = jnp.take(slab_b, month_block, axis=0)

    partial_y = jnp.einsum("tijc,cr->tijr", tile_values, slab_c, preferred_element_type=jnp.float32)
    contrib = jnp.sum(partial_y * picked_b[:, None, :, :], axis=2)
    selector = (prov_block[:, None] == jnp.arange(PB_DEV, dtype=jnp.int32)[None, :]).astype(jnp.float32)
    partial_a = jnp.einsum("tp,tir->pir", selector, contrib, precision=HIGH)

    pair_a = lax.all_to_all(partial_a.reshape(n_month, n_bin, tile_i, rank), "month", 0, 0, tiled=True)
    pair_a = jnp.sum(pair_a, axis=0)
    own_a = lax.all_to_all(pair_a, "bin", 0, 0, tiled=True)
    own_a = jnp.sum(own_a, axis=0)

    float_b = whole_b.astype(jnp.float32)
    float_c = whole_c.astype(jnp.float32)
    gram_b = dot32(float_b, float_b, ((0,), (0,)))
    gram_c = dot32(float_c, float_c, ((0,), (0,)))
    factor_a = apply_inverse(own_a, inverse_factor(gram_b * gram_c))

    slab_a = lax.all_to_all(
        jnp.broadcast_to(factor_a[None], (n_month * n_bin,) + factor_a.shape), ("month", "bin"), 0, 0, tiled=True
    )
    flat_a = slab_a.reshape(-1, rank)
    slab_gram = dot32(flat_a, flat_a, ((0,), (0,)))
    slab_gram = jnp.concatenate([slab_gram[: rank // 2], slab_gram[rank // 2 :]], axis=1)
    grams = lax.all_to_all(jnp.broadcast_to(slab_gram[None], (n_prov,) + slab_gram.shape), "prov", 0, 0, tiled=True)
    gram = jnp.sum(grams, axis=0)
    gram = jnp.concatenate([gram[:, :rank], gram[:, rank:]], axis=0)
    scale = jnp.sqrt(jnp.diagonal(gram) + epsilon)
    gram_a = gram / scale[:, None] / scale[None, :]

    high = slab_a.astype(jnp.bfloat16)
    low = (slab_a - high.astype(jnp.float32)).astype(jnp.bfloat16)
    both = jnp.concatenate([high, low], axis=2)
    picked_a = jnp.take(both, prov_block, axis=0)
    partial_w = jnp.einsum("tijc,tir->tjcr", tile_values, picked_a, preferred_element_type=jnp.float32)
    twice_b = jnp.concatenate([picked_b, picked_b], axis=2)
    partial_c = jnp.sum(partial_w * twice_b[:, :, None, :], axis=(0, 1))
    partial_c = partial_c[:, :rank] + partial_c[:, rank:]
    out_rows = tile_k // (n_prov * n_month)
    own_c = lax.all_to_all(
        partial_c.reshape(n_prov * n_month, 1, out_rows * rank), ("prov", "month"), 0, 0, tiled=True
    )
    own_c = jnp.sum(own_c, axis=0).reshape(out_rows, rank) / scale[None, :]
    new_c = apply_inverse(own_c, inverse_factor(gram_a * gram_b))
    return (factor_a, new_c)


def solution(mesh):
    in_specs = (
        P(("prov", "month", "bin"), None, None, None),
        P(("prov", "month", "bin")),
        P(("prov", "month", "bin")),
        P(("prov", "month"), None),
        P(("prov", "bin"), None),
    )
    out_specs = (P(("prov", "month", "bin"), None), P(("bin", "prov", "month"), None))
    return jax.shard_map(shards, mesh=mesh, in_specs=in_specs, out_specs=out_specs, check_vma=False)
```

```python
import jax
import jax.numpy as jnp
from jax import lax
from jax.experimental import pallas as pl
from jax.experimental.pallas import tpu as pltpu
from jax.sharding import PartitionSpec as P

MB_DEV = 8
PB_DEV = 16
epsilon = 1e-06
HIGH = lax.Precision.HIGHEST


def dot32(a, b, dims, precision=HIGH):
    return lax.dot_general(a, b, (dims, ((), ())), precision=precision, preferred_element_type=jnp.float32)


def spd_inverse(a):
    n = a.shape[0]
    lane = lax.broadcasted_iota(jnp.int32, a.shape, 1)
    sub = lax.broadcasted_iota(jnp.int32, a.shape, 0)
    lane_row = lax.broadcasted_iota(jnp.int32, (1, n), 1)
    for k in range(n):
        col = a[:, k : k + 1]
        inv = 1.0 / a[k : k + 1, k : k + 1]
        row = jnp.where(lane_row == k, inv, a[k : k + 1, :] * inv)
        rest = jnp.where(lane == k, 0.0, a) - col * row
        a = jnp.where(sub == k, row, rest)
    return a


def first_inverse_kernel(b_ref, pairs_ref, inv_ref, gram_b_ref):
    rank = b_ref.shape[1]
    b = b_ref[...]
    gram_b = dot32(b, b, ((0,), (0,)), None)
    z = pairs_ref[...]
    twin = dot32(z, z, ((0,), (0,)), None)
    gram_c = twin[:rank, :rank] + twin[rank:, rank:]
    gram_b_ref[...] = gram_b
    inv_ref[...] = spd_inverse(gram_b * gram_c)


def last_kernel(got_ref, gram_b_ref, out_ref):
    rank = gram_b_ref.shape[0]
    rows = jnp.sum(got_ref[:, 0, :], axis=0, keepdims=True)
    own = jnp.concatenate([rows[:, :rank], rows[:, rank:]], axis=0)
    gram = got_ref[:, 1, :rank]
    lane = lax.broadcasted_iota(jnp.int32, gram.shape, 1)
    sub = lax.broadcasted_iota(jnp.int32, gram.shape, 0)
    diag = jnp.where(lane == sub, gram, 0.0)
    scale_row = jnp.sqrt(jnp.sum(diag, axis=0, keepdims=True) + epsilon)
    scale_col = jnp.sqrt(jnp.sum(diag, axis=1, keepdims=True) + epsilon)
    system = gram / scale_col / scale_row * gram_b_ref[...]
    out_ref[...] = dot32(own / scale_row, spd_inverse(system), ((1,), (0,)))


def pick(blocks, index):
    return blocks.at[index].get(mode="promise_in_bounds")


def shards(tile_values, prov_block, month_block, factor_b, factor_c):
    tiles, tile_i, tile_j, tile_k = tile_values.shape
    rank = factor_b.shape[1]
    n_prov = lax.axis_size("prov")
    n_month = lax.axis_size("month")
    n_bin = lax.axis_size("bin")
    month = lax.axis_index("month")
    bin_at = lax.axis_index("bin")

    n_all = n_prov * n_month * n_bin
    c_rows = factor_c.shape[0] // n_month
    b_rep = n_bin // factor_b.shape[0]
    own_c_rows = lax.dynamic_slice_in_dim(factor_c, month * c_rows, c_rows, 0).reshape(1, c_rows * rank)
    own_b_row = lax.dynamic_slice_in_dim(factor_b, bin_at // b_rep, 1, 0)
    own_b_row = jnp.concatenate([own_b_row] * c_rows, axis=1)
    chunk = jnp.concatenate([own_c_rows, own_b_row], axis=0)
    sent = jnp.broadcast_to(chunk[None], (n_all,) + chunk.shape)
    got = lax.all_to_all(sent, ("prov", "bin", "month"), 0, 0, tiled=True)
    pairs_c = got[:, 0, :]
    whole_b = got[:, 1, :rank].reshape(n_prov, factor_b.shape[0], b_rep, n_month, rank)[:, :, 0]
    whole_b = whole_b.transpose(0, 2, 1, 3).reshape(-1, rank)

    slab_pairs = lax.dynamic_slice_in_dim(pairs_c, bin_at * (tile_k // c_rows), tile_k // c_rows, 0)
    slab_c = slab_pairs.reshape(tile_k, rank)
    slab_b = lax.dynamic_slice_in_dim(whole_b, month * (MB_DEV * tile_j), MB_DEV * tile_j, 0)
    slab_b = slab_b.astype(jnp.float32).reshape(MB_DEV, tile_j, rank)
    picked_b = pick(slab_b, month_block)

    partial_y = jnp.einsum("tijc,cr->tijr", tile_values, slab_c, preferred_element_type=jnp.float32)
    contrib = jnp.sum(partial_y * picked_b[:, None, :, :], axis=2)
    selector = (prov_block[:, None] == jnp.arange(PB_DEV, dtype=jnp.int32)[None, :]).astype(jnp.float32)
    partial_a = jnp.einsum("tp,tir->pir", selector, contrib, precision=HIGH)

    pair_a = lax.all_to_all(partial_a.reshape(n_month, n_bin, tile_i, rank), "month", 0, 0, tiled=True)
    pair_a = jnp.sum(pair_a, axis=0)
    whole_b, pairs_c, pair_a = lax.optimization_barrier((whole_b, pairs_c, pair_a))
    own_a = lax.all_to_all(pair_a, "bin", 0, 0, tiled=True)

    square = jax.ShapeDtypeStruct((rank, rank), jnp.float32)
    inverse, gram_b = pl.pallas_call(
        first_inverse_kernel,
        out_shape=(square, square),
        cost_estimate=pl.CostEstimate(flops=20000000, bytes_accessed=200000, transcendentals=0),
        name="first_inverse",
    )(whole_b, pairs_c)
    own_a = jnp.sum(own_a, axis=0)
    factor_a = dot32(own_a, inverse, ((1,), (0,)))

    half_a = lax.all_to_all(jnp.broadcast_to(factor_a[None], (n_bin,) + factor_a.shape), "bin", 0, 0, tiled=True)
    flat_a = half_a.reshape(-1, rank)
    half_gram = dot32(flat_a, flat_a, ((0,), (0,)))
    gram_rows = lax.all_to_all(half_gram.reshape(rank, 1, rank), ("prov", "month"), 0, 0, tiled=True)

    other_a = lax.ppermute(half_a, "month", [(i, n_month - 1 - i) for i in range(n_month)])

    def split(values):
        high = lax.reduce_precision(values, 8, 7)
        return jnp.concatenate([high, values - high], axis=2).astype(jnp.bfloat16)

    both = jnp.concatenate([split(half_a), split(other_a)], axis=0)
    picked_a = pick(both, prov_block ^ (month * n_bin))
    partial_w = jnp.einsum("tijc,tir->tjcr", tile_values, picked_a, preferred_element_type=jnp.float32)
    twice_b = jnp.concatenate([picked_b, picked_b], axis=2)
    partial_c = jnp.sum(partial_w * twice_b[:, :, None, :], axis=(0, 1))
    partial_c = partial_c[:, :rank] + partial_c[:, rank:]

    gram_rows, partial_c = lax.optimization_barrier((gram_rows, partial_c))
    gram_row = jnp.sum(gram_rows, axis=0)
    n_out = n_prov * n_month
    out_rows = tile_k // n_out
    sent_c = partial_c.reshape(n_out, 1, out_rows * rank)
    sent_row = jnp.broadcast_to(jnp.concatenate([gram_row] * out_rows, axis=1)[None], sent_c.shape)
    last = lax.all_to_all(jnp.concatenate([sent_c, sent_row], axis=1), ("prov", "month"), 0, 0, tiled=True)
    new_c = pl.pallas_call(
        last_kernel, out_shape=jax.ShapeDtypeStruct((out_rows, rank), jnp.float32), name="last_solve"
    )(last, gram_b)
    return (factor_a, new_c)


def solution(mesh):
    in_specs = (
        P(("prov", "month", "bin"), None, None, None),
        P(("prov", "month", "bin")),
        P(("prov", "month", "bin")),
        P(("prov", "month"), None),
        P(("prov", "bin"), None),
    )
    out_specs = (P(("prov", "month", "bin"), None), P(("bin", "prov", "month"), None))
    return jax.shard_map(shards, mesh=mesh, in_specs=in_specs, out_specs=out_specs, check_vma=False)
```

```python
import jax
import jax.numpy as jnp
from jax import lax
from jax.experimental import pallas as pl
from jax.experimental.pallas import tpu as pltpu
from jax.sharding import PartitionSpec as P

MB_DEV = 8
PB_DEV = 16
epsilon = 1e-06
HIGH = lax.Precision.HIGHEST
SMALL = pltpu.CompilerParams(vmem_limit_bytes=8 * 1024 * 1024)
PROV = ("zl", "y")
BIN = ("x", "zh")
GRAM = ("zl", "month")


def dot32(a, b, dims, precision=HIGH):
    return lax.dot_general(a, b, (dims, ((), ())), precision=precision, preferred_element_type=jnp.float32)


def diagonals(a):
    lane = lax.broadcasted_iota(jnp.int32, a.shape, 1)
    sub = lax.broadcasted_iota(jnp.int32, a.shape, 0)
    diag = jnp.where(lane == sub, a, 0.0)
    return jnp.sum(diag, axis=0, keepdims=True), jnp.sum(diag, axis=1, keepdims=True)


def spd_inverse(a):
    n = a.shape[0]
    in_row, in_col = diagonals(a)
    in_row, in_col = lax.rsqrt(in_row), lax.rsqrt(in_col)
    a = a * in_col * in_row
    lane = lax.broadcasted_iota(jnp.int32, a.shape, 1)
    sub = lax.broadcasted_iota(jnp.int32, a.shape, 0)
    lane_row = lax.broadcasted_iota(jnp.int32, (1, n), 1)
    for k in range(0, n, 2):
        col0 = jnp.broadcast_to(a[:, k : k + 1], a.shape)
        col1 = jnp.broadcast_to(a[:, k + 1 : k + 2], a.shape)
        p, q, s = col0[k : k + 1], col1[k : k + 1], col1[k + 1 : k + 2]
        inv = 1.0 / (p * s - q * q)
        p, q, s = p * inv, q * inv, s * inv
        row0, row1 = a[k : k + 1], a[k + 1 : k + 2]
        first, second = lane_row == k, lane_row == k + 1
        new0 = jnp.where(first, s, jnp.where(second, -q, s * row0 - q * row1))
        new1 = jnp.where(first, -q, jnp.where(second, p, p * row1 - q * row0))
        rest = jnp.where((lane == k) | (lane == k + 1), 0.0, a) - col0 * new0 - col1 * new1
        a = jnp.where(sub == k, new0, jnp.where(sub == k + 1, new1, rest))
    return a * in_col * in_row


def first_inverse_kernel(b_ref, pairs_ref, inv_ref, gram_b_ref):
    rank = b_ref.shape[1]
    b = b_ref[...]
    gram_b = dot32(b, b, ((0,), (0,)), None)
    z = pairs_ref[...]
    twin = dot32(z, z, ((0,), (0,)), None)
    gram_c = twin[:rank, :rank] + twin[rank:, rank:]
    gram_b_ref[...] = gram_b
    inv_ref[...] = spd_inverse(gram_b * gram_c)


def gram_kernel(a_ref, out_ref):
    rank = a_ref.shape[1]
    gram = dot32(a_ref[0], a_ref[0], ((1,), (1,)))
    for block in range(1, a_ref.shape[0]):
        gram = gram + dot32(a_ref[block], a_ref[block], ((1,), (1,)))
    groups = out_ref.shape[0]
    for j in range(rank // groups):
        out_ref[:, j * rank : (j + 1) * rank] = gram[j * groups : (j + 1) * groups]


def last_kernel(got_ref, gram_b_ref, out_ref):
    rank = gram_b_ref.shape[0]
    width = got_ref.shape[1]
    lead = out_ref.shape[0] * rank
    groups = rank * rank // (width - lead)
    got = got_ref[...]
    rows = jnp.sum(got[:, :lead], axis=0, keepdims=True)
    own = jnp.concatenate([rows[:, j * rank : (j + 1) * rank] for j in range(out_ref.shape[0])], axis=0)
    folded = got[:groups, lead:]
    for part in range(1, got.shape[0] // groups):
        folded = folded + got[part * groups : (part + 1) * groups, lead:]
    gram = jnp.concatenate([folded[:, j * rank : (j + 1) * rank] for j in range(rank // groups)], axis=0)
    square_row, square_col = diagonals(gram)
    scale_row = jnp.sqrt(square_row + epsilon)
    scale_col = jnp.sqrt(square_col + epsilon)
    system = gram / scale_col / scale_row * gram_b_ref[...]
    out_ref[...] = dot32(own / scale_row, spd_inverse(system), ((1,), (0,)))


def pick(blocks, index):
    return blocks.at[index].get(mode="promise_in_bounds")


def shards(tile_values, prov_block, month_block, factor_b, factor_c):
    tiles, tile_i, tile_j, tile_k = tile_values.shape
    rank = factor_b.shape[1]
    n_prov = lax.axis_size(PROV)
    n_month = lax.axis_size("month")
    n_bin = lax.axis_size(BIN)
    month = lax.axis_index("month")
    bin_at = lax.axis_index(BIN)

    n_all = n_prov * n_month * n_bin
    c_rows = factor_c.shape[0] // n_month
    b_rep = n_bin // factor_b.shape[0]
    own_c_rows = lax.dynamic_slice_in_dim(factor_c, month * c_rows, c_rows, 0).reshape(1, c_rows * rank)
    own_b_row = lax.dynamic_slice_in_dim(factor_b, bin_at // b_rep, 1, 0)
    own_b_row = jnp.concatenate([own_b_row] * c_rows, axis=1)
    chunk = jnp.concatenate([own_c_rows, own_b_row], axis=0)
    sent = jnp.broadcast_to(chunk[None], (n_all,) + chunk.shape)
    got = lax.all_to_all(sent, PROV + BIN + ("month",), 0, 0, tiled=True)
    pairs_c = got[:, 0, :]
    whole_b = got[:, 1, :rank].reshape(n_prov, factor_b.shape[0], b_rep, n_month, rank)[:, :, 0]
    whole_b = whole_b.transpose(0, 2, 1, 3).reshape(-1, rank)

    slab_pairs = lax.dynamic_slice_in_dim(pairs_c, bin_at * (tile_k // c_rows), tile_k // c_rows, 0)
    slab_c = slab_pairs.reshape(tile_k, rank)
    slab_b = lax.dynamic_slice_in_dim(whole_b, month * (MB_DEV * tile_j), MB_DEV * tile_j, 0)
    slab_b = slab_b.astype(jnp.float32).reshape(MB_DEV, tile_j, rank)
    picked_b = pick(slab_b, month_block)

    partial_y = jnp.einsum("tijc,cr->tijr", tile_values, slab_c, preferred_element_type=jnp.float32)
    contrib = jnp.sum(partial_y * picked_b[:, None, :, :], axis=2)
    selector = (prov_block[:, None] == jnp.arange(PB_DEV, dtype=jnp.int32)[None, :]).astype(jnp.float32)
    partial_a = jnp.einsum("tp,tir->pir", selector, contrib, precision=HIGH)

    pair_a = lax.all_to_all(partial_a.reshape(n_month, n_bin, tile_i, rank), "month", 0, 0, tiled=True)
    pair_a = jnp.sum(pair_a, axis=0)
    whole_b, pairs_c, pair_a = lax.optimization_barrier((whole_b, pairs_c, pair_a))
    own_a = lax.all_to_all(pair_a, BIN, 0, 0, tiled=True)

    square = jax.ShapeDtypeStruct((rank, rank), jnp.float32)
    inverse, gram_b = pl.pallas_call(
        first_inverse_kernel,
        out_shape=(square, square),
        cost_estimate=pl.CostEstimate(flops=20000000, bytes_accessed=200000, transcendentals=0),
        name="first_inverse",
        compiler_params=SMALL,
    )(whole_b, pairs_c)
    own_a = jnp.sum(own_a, axis=0)
    factor_a = dot32(own_a, inverse, ((1,), (0,)))

    half_a = lax.all_to_all(jnp.broadcast_to(factor_a[None], (n_bin,) + factor_a.shape), BIN, 0, 0, tiled=True)
    n_gram = lax.axis_size(GRAM)
    half_gram = pl.pallas_call(
        gram_kernel, out_shape=jax.ShapeDtypeStruct((n_gram, rank * rank // n_gram), jnp.float32), name="half_gram", compiler_params=SMALL
    )(half_a.transpose(0, 2, 1))
    gram_rows = lax.all_to_all(half_gram[:, None, :], GRAM, 0, 0, tiled=True)

    other_a = lax.ppermute(half_a, "month", [(i, n_month - 1 - i) for i in range(n_month)])

    def split(values):
        high = lax.reduce_precision(values, 8, 7)
        return jnp.concatenate([high, values - high], axis=2).astype(jnp.bfloat16)

    both = jnp.concatenate([split(half_a), split(other_a)], axis=0)
    picked_a = pick(both, prov_block ^ (month * n_bin))
    partial_w = jnp.einsum("tijc,tir->tjcr", tile_values, picked_a, preferred_element_type=jnp.float32)
    twice_b = jnp.concatenate([picked_b, picked_b], axis=2)
    partial_c = jnp.sum(partial_w * twice_b[:, :, None, :], axis=(0, 1))
    partial_c = partial_c[:, :rank] + partial_c[:, rank:]

    gram_rows, partial_c = lax.optimization_barrier((gram_rows, partial_c))
    gram_row = jnp.sum(gram_rows, axis=0, keepdims=True)
    n_out = n_prov * n_month
    out_rows = tile_k // n_out
    n_y = lax.axis_size("y")
    sent_c = partial_c.reshape(n_prov // n_y, n_y, n_month, out_rows * rank).transpose(1, 0, 2, 3)
    sent_c = sent_c.reshape(n_out, 1, out_rows * rank)
    sent_row = jnp.broadcast_to(gram_row, (n_out,) + gram_row.shape[1:])
    last = lax.all_to_all(jnp.concatenate([sent_c, sent_row], axis=2), ("y",) + GRAM, 0, 0, tiled=True)
    new_c = pl.pallas_call(
        last_kernel, out_shape=jax.ShapeDtypeStruct((out_rows, rank), jnp.float32), name="last_solve", compiler_params=SMALL
    )(last.reshape(n_out, -1), gram_b)
    return (factor_a, new_c)


def solution(mesh):
    prov, month, bins = mesh.devices.shape
    shape = (prov // 8, 8, month, bins // 2, 2)
    mesh = jax.sharding.Mesh(mesh.devices.reshape(shape), ("zl", "y", "month", "x", "zh"))
    everywhere = PROV + ("month",) + BIN
    in_specs = (
        P(everywhere, None, None, None),
        P(everywhere),
        P(everywhere),
        P(PROV + ("month",), None),
        P(PROV + BIN, None),
    )
    out_specs = (P(everywhere, None), P(BIN + PROV + ("month",), None))
    return jax.shard_map(shards, mesh=mesh, in_specs=in_specs, out_specs=out_specs, check_vma=False)
```

```python
import jax
import jax.numpy as jnp
from jax import lax
from jax.experimental import pallas as pl
from jax.experimental.pallas import tpu as pltpu
from jax.sharding import PartitionSpec as P

MB_DEV = 8
PB_DEV = 16
epsilon = 1e-06
HIGH = lax.Precision.HIGHEST
SMALL = pltpu.CompilerParams(vmem_limit_bytes=8 * 1024 * 1024)
LARGE = pltpu.CompilerParams(vmem_limit_bytes=52 * 1024 * 1024)
PROV = ("zl", "y")
BIN = ("x", "zh")
GRAM = ("zl", "month")


def dot32(a, b, dims, precision=HIGH):
    return lax.dot_general(a, b, (dims, ((), ())), precision=precision, preferred_element_type=jnp.float32)


def diagonals(a):
    lane = lax.broadcasted_iota(jnp.int32, a.shape, 1)
    sub = lax.broadcasted_iota(jnp.int32, a.shape, 0)
    diag = jnp.where(lane == sub, a, 0.0)
    return jnp.sum(diag, axis=0, keepdims=True), jnp.sum(diag, axis=1, keepdims=True)


def spd_inverse(a):
    n = a.shape[0]
    in_row, in_col = diagonals(a)
    in_row, in_col = lax.rsqrt(in_row), lax.rsqrt(in_col)
    a = a * in_col * in_row
    lane = lax.broadcasted_iota(jnp.int32, a.shape, 1)
    sub = lax.broadcasted_iota(jnp.int32, a.shape, 0)
    lane_row = lax.broadcasted_iota(jnp.int32, (1, n), 1)
    for k in range(0, n, 2):
        col0 = jnp.broadcast_to(a[:, k : k + 1], a.shape)
        col1 = jnp.broadcast_to(a[:, k + 1 : k + 2], a.shape)
        p, q, s = col0[k : k + 1], col1[k : k + 1], col1[k + 1 : k + 2]
        inv = 1.0 / (p * s - q * q)
        p, q, s = p * inv, q * inv, s * inv
        row0, row1 = a[k : k + 1], a[k + 1 : k + 2]
        first, second = lane_row == k, lane_row == k + 1
        new0 = jnp.where(first, s, jnp.where(second, -q, s * row0 - q * row1))
        new1 = jnp.where(first, -q, jnp.where(second, p, p * row1 - q * row0))
        rest = jnp.where((lane == k) | (lane == k + 1), 0.0, a) - col0 * new0 - col1 * new1
        a = jnp.where(sub == k, new0, jnp.where(sub == k + 1, new1, rest))
    return a * in_col * in_row


def first_inverse_kernel(b_ref, pairs_ref, inv_ref, gram_b_ref):
    rank = inv_ref.shape[0]
    b = b_ref[:, :rank]
    gram_b = dot32(b, b, ((0,), (0,)), None)
    z = pairs_ref[...]
    twin = dot32(z, z, ((0,), (0,)), None)
    gram_c = twin[:rank, :rank] + twin[rank:, rank:]
    gram_b_ref[...] = gram_b
    inv_ref[...] = spd_inverse(gram_b * gram_c)


def tile_copies(tiles_ref, held, sems):
    copies = [pltpu.make_async_copy(tiles_ref.at[t], held.at[t], sems.at[t]) for t in range(held.shape[0])]
    for copy in copies:
        copy.start()
    return copies


def both_halves(held, t):
    _, tile_i, tile_j, tile_k = held.shape
    half = tile_i // 2
    upper = held[t, :half].reshape(half * tile_j, tile_k)
    lower = held[t, half:].reshape(half * tile_j, tile_k)
    return jnp.concatenate([upper, lower], axis=1)


def first_product_kernel(prov_ref, month_ref, tiles_ref, c_ref, b_ref, out_ref, held, sems):
    copies = tile_copies(tiles_ref, held, sems)
    out_ref[...] = jnp.zeros_like(out_ref)
    c = c_ref[...]
    zero = jnp.zeros_like(c)
    twice_c = jnp.concatenate([jnp.concatenate([c, zero], axis=1), jnp.concatenate([zero, c], axis=1)], axis=0)
    half, tile_j = held.shape[1] // 2, held.shape[2]
    for t in range(held.shape[0]):
        copies[t].wait()
        product = dot32(both_halves(held, t), twice_c, ((1,), (0,)), None)
        product = product.reshape(half, tile_j, -1) * b_ref[month_ref[t]][None]
        out_ref[prov_ref[t]] += jnp.sum(product, axis=1)


def solve_kernel(got_ref, inv_ref, out_ref, own_ref):
    rank = inv_ref.shape[0]
    total = got_ref[0]
    for source in range(1, got_ref.shape[0]):
        total = total + got_ref[source]
    inv = inv_ref[...]
    upper = dot32(total[:, :rank], inv, ((1,), (0,)))
    lower = dot32(total[:, rank:], inv, ((1,), (0,)))
    solved = jnp.concatenate([upper, lower], axis=1)
    for target in range(out_ref.shape[0]):
        out_ref[target] = solved
    own_ref[: upper.shape[0]] = upper
    own_ref[upper.shape[0] :] = lower


def gram_kernel(a_ref, out_ref):
    rank = a_ref.shape[2] // 2
    rows = a_ref[...].reshape(-1, 2 * rank)
    twin = dot32(rows, rows, ((0,), (0,)))
    gram = twin[:rank, :rank] + twin[rank:, rank:]
    groups = out_ref.shape[0]
    for j in range(rank // groups):
        out_ref[:, j * rank : (j + 1) * rank] = gram[j * groups : (j + 1) * groups]


def last_product_kernel(at_ref, month_ref, tiles_ref, a_ref, other_ref, b_ref, out_ref, held, sems, turned):
    copies = tile_copies(tiles_ref, held, sems)
    blocks, half, lanes = a_ref.shape
    rank, tile_j, tile_k = lanes // 2, held.shape[2], held.shape[3]
    total = None
    for t in range(held.shape[0]):
        at = at_ref[t]
        a = jnp.where(at < blocks, a_ref[at % blocks], other_ref[at % blocks])
        joint = (a[:, None, :] * b_ref[month_ref[t]][None]).reshape(half * tile_j, lanes)
        high = joint.astype(jnp.bfloat16)
        low = (joint - high.astype(jnp.float32)).astype(jnp.bfloat16)
        copies[t].wait()
        part = dot32(jnp.concatenate([high, low], axis=1), both_halves(held, t), ((0,), (0,)), None)
        total = part if total is None else total + part
    parts = [total[k * rank : (k + 1) * rank, (k % 2) * tile_k : (k % 2 + 1) * tile_k] for k in range(4)]
    turned[...] = (parts[0] + parts[1] + parts[2] + parts[3]).T
    out_rows = lanes // rank
    for row in range(out_rows):
        out_ref[:, row * rank : (row + 1) * rank] = turned[pl.ds(row, tile_k // out_rows, stride=out_rows), :]


def last_kernel(got_ref, gram_b_ref, out_ref):
    rank = gram_b_ref.shape[0]
    width = got_ref.shape[1]
    lead = out_ref.shape[0] * rank
    groups = rank * rank // (width - lead)
    got = got_ref[...]
    rows = jnp.sum(got[:, :lead], axis=0, keepdims=True)
    own = jnp.concatenate([rows[:, j * rank : (j + 1) * rank] for j in range(out_ref.shape[0])], axis=0)
    n_zl = groups // 2
    per = got.shape[0] // n_zl
    folded = []
    for zl in range(n_zl):
        part = jnp.sum(got[zl * per : (zl + 1) * per, lead:].reshape(per // 8, 8, width - lead), axis=0)
        folded.append((part[0:2] + part[2:4]) + (part[4:6] + part[6:8]))
    folded = jnp.concatenate(folded, axis=0)
    gram = jnp.concatenate([folded[:, j * rank : (j + 1) * rank] for j in range(rank // groups)], axis=0)
    square_row, square_col = diagonals(gram)
    scale_row = jnp.sqrt(square_row + epsilon)
    scale_col = jnp.sqrt(square_col + epsilon)
    system = gram / scale_col / scale_row * gram_b_ref[...]
    out_ref[...] = dot32(own / scale_row, spd_inverse(system), ((1,), (0,)))


def shards(tile_values, prov_block, month_block, factor_b, factor_c):
    tiles, tile_i, tile_j, tile_k = tile_values.shape
    rank = factor_b.shape[1]
    n_prov = lax.axis_size(PROV)
    n_month = lax.axis_size("month")
    n_bin = lax.axis_size(BIN)
    month = lax.axis_index("month")
    bin_at = lax.axis_index(BIN)

    n_all = n_prov * n_month * n_bin
    c_rows = factor_c.shape[0] // n_month
    b_rep = n_bin // factor_b.shape[0]
    own_c_rows = lax.dynamic_slice_in_dim(factor_c, month * c_rows, c_rows, 0).reshape(1, c_rows * rank)
    own_b_row = lax.dynamic_slice_in_dim(factor_b, bin_at // b_rep, 1, 0)
    own_b_row = jnp.concatenate([own_b_row] * c_rows, axis=1)
    chunk = jnp.concatenate([own_c_rows, own_b_row], axis=0)
    sent = jnp.broadcast_to(chunk[None], (n_all,) + chunk.shape)
    got = lax.all_to_all(sent, PROV + BIN + ("month",), 0, 0, tiled=True)
    pairs_c = got[:, 0, :]
    twice_b = got[:, 1, :].reshape(n_prov, factor_b.shape[0], b_rep, n_month, c_rows * rank)[:, :, 0]
    twice_b = twice_b.transpose(0, 2, 1, 3).reshape(-1, c_rows * rank)

    slab_pairs = lax.dynamic_slice_in_dim(pairs_c, bin_at * (tile_k // c_rows), tile_k // c_rows, 0)
    slab_c = slab_pairs.reshape(tile_k, rank)
    slab_b = lax.dynamic_slice_in_dim(twice_b, month * (MB_DEV * tile_j), MB_DEV * tile_j, 0)
    slab_b = slab_b.astype(jnp.float32).reshape(MB_DEV, tile_j, c_rows * rank)

    smem, vmem, hbm = (pl.BlockSpec(memory_space=space) for space in (pltpu.SMEM, pltpu.VMEM, pl.ANY))
    tile_scratch = [pltpu.VMEM(tile_values.shape, tile_values.dtype), pltpu.SemaphoreType.DMA((tiles,))]
    half = tile_i // 2
    partial_a = pl.pallas_call(
        first_product_kernel,
        out_shape=jax.ShapeDtypeStruct((PB_DEV, half, 2 * rank), jnp.float32),
        in_specs=[smem, smem, hbm, vmem, vmem],
        out_specs=vmem,
        scratch_shapes=tile_scratch,
        compiler_params=LARGE,
        name="first_product",
    )(prov_block, month_block, tile_values, slab_c, slab_b)

    pair_a = lax.all_to_all(partial_a.reshape(n_month, n_bin, half, 2 * rank), "month", 0, 0, tiled=True)
    pair_a = jnp.sum(pair_a, axis=0)
    twice_b, pairs_c, pair_a = lax.optimization_barrier((twice_b, pairs_c, pair_a))
    own_a = lax.all_to_all(pair_a, BIN, 0, 0, tiled=True)

    square = jax.ShapeDtypeStruct((rank, rank), jnp.float32)
    inverse, gram_b = pl.pallas_call(
        first_inverse_kernel,
        out_shape=(square, square),
        cost_estimate=pl.CostEstimate(flops=20000000, bytes_accessed=200000, transcendentals=0),
        name="first_inverse",
        compiler_params=SMALL,
    )(twice_b, pairs_c)
    spread, factor_a = pl.pallas_call(
        solve_kernel,
        out_shape=(
            jax.ShapeDtypeStruct(own_a.shape, jnp.float32),
            jax.ShapeDtypeStruct((tile_i, rank), jnp.float32),
        ),
        compiler_params=SMALL,
        name="solve_first",
    )(own_a, inverse)

    half_a = lax.all_to_all(spread, BIN, 0, 0, tiled=True)
    n_gram = lax.axis_size(GRAM)
    half_gram = pl.pallas_call(
        gram_kernel,
        out_shape=jax.ShapeDtypeStruct((n_gram, rank * rank // n_gram), jnp.float32),
        compiler_params=SMALL,
        name="half_gram",
    )(half_a)
    gram_rows = lax.all_to_all(half_gram[:, None, :], GRAM, 0, 0, tiled=True)

    other_a = lax.ppermute(half_a, "month", [(i, n_month - 1 - i) for i in range(n_month)])

    n_out = n_prov * n_month
    out_rows = tile_k // n_out
    partial_c = pl.pallas_call(
        last_product_kernel,
        out_shape=jax.ShapeDtypeStruct((n_out, out_rows * rank), jnp.float32),
        in_specs=[smem, smem, hbm, vmem, vmem, vmem],
        out_specs=vmem,
        scratch_shapes=tile_scratch + [pltpu.VMEM((tile_k, rank), jnp.float32)],
        compiler_params=LARGE,
        name="last_product",
    )(prov_block ^ (month * n_bin), month_block, tile_values, half_a, other_a, slab_b)

    gram_rows, partial_c = lax.optimization_barrier((gram_rows, partial_c))
    gram_row = jnp.sum(gram_rows, axis=0, keepdims=True)
    sent_row = jnp.broadcast_to(gram_row, (n_out,) + gram_row.shape[1:])
    last = jnp.concatenate([partial_c[:, None, :], sent_row], axis=2)
    last = lax.all_to_all(last, PROV + ("month",), 0, 0, tiled=True)
    new_c = pl.pallas_call(
        last_kernel,
        out_shape=jax.ShapeDtypeStruct((out_rows, rank), jnp.float32),
        compiler_params=SMALL,
        name="last_solve",
    )(last.reshape(n_out, -1), gram_b)
    return (factor_a, new_c)


def solution(mesh):
    prov, month, bins = mesh.devices.shape
    shape = (prov // 8, 8, month, bins // 2, 2)
    mesh = jax.sharding.Mesh(mesh.devices.reshape(shape), ("zl", "y", "month", "x", "zh"))
    everywhere = PROV + ("month",) + BIN
    in_specs = (
        P(everywhere, None, None, None),
        P(everywhere),
        P(everywhere),
        P(PROV + ("month",), None),
        P(PROV + BIN, None),
    )
    out_specs = (P(everywhere, None), P(BIN + PROV + ("month",), None))
    return jax.shard_map(shards, mesh=mesh, in_specs=in_specs, out_specs=out_specs, check_vma=False)
```

```python
import jax
import jax.numpy as jnp
from jax import lax
from jax.experimental import pallas as pl
from jax.experimental.pallas import tpu as pltpu
from jax.sharding import PartitionSpec as P

MB_DEV = 8
KEPT = 5
PB_DEV = 16
epsilon = 1e-06
HIGH = lax.Precision.HIGHEST
SMALL = pltpu.CompilerParams(vmem_limit_bytes=8 * 1024 * 1024)
LARGE = pltpu.CompilerParams(vmem_limit_bytes=50 * 1024 * 1024)
PROV = ("zl", "y")
BIN = ("x", "zh")
GRAM = ("zl", "month")


def dot32(a, b, dims, precision=HIGH):
    return lax.dot_general(a, b, (dims, ((), ())), precision=precision, preferred_element_type=jnp.float32)


def diagonals(a):
    lane = lax.broadcasted_iota(jnp.int32, a.shape, 1)
    sub = lax.broadcasted_iota(jnp.int32, a.shape, 0)
    diag = jnp.where(lane == sub, a, 0.0)
    return jnp.sum(diag, axis=0, keepdims=True), jnp.sum(diag, axis=1, keepdims=True)


def spd_inverse(a):
    n = a.shape[0]
    in_row, in_col = diagonals(a)
    in_row, in_col = lax.rsqrt(in_row), lax.rsqrt(in_col)
    a = a * in_col * in_row
    lane = lax.broadcasted_iota(jnp.int32, a.shape, 1)
    sub = lax.broadcasted_iota(jnp.int32, a.shape, 0)
    lane_row = lax.broadcasted_iota(jnp.int32, (1, n), 1)
    for k in range(0, n, 2):
        col0 = jnp.broadcast_to(a[:, k : k + 1], a.shape)
        col1 = jnp.broadcast_to(a[:, k + 1 : k + 2], a.shape)
        p, q, s = col0[k : k + 1], col1[k : k + 1], col1[k + 1 : k + 2]
        inv = 1.0 / (p * s - q * q)
        p, q, s = p * inv, q * inv, s * inv
        row0, row1 = a[k : k + 1], a[k + 1 : k + 2]
        first, second = lane_row == k, lane_row == k + 1
        new0 = jnp.where(first, s, jnp.where(second, -q, s * row0 - q * row1))
        new1 = jnp.where(first, -q, jnp.where(second, p, p * row1 - q * row0))
        rest = jnp.where((lane == k) | (lane == k + 1), 0.0, a) - col0 * new0 - col1 * new1
        a = jnp.where(sub == k, new0, jnp.where(sub == k + 1, new1, rest))
    return a * in_col * in_row


def first_inverse_kernel(b_ref, pairs_ref, inv_ref, gram_b_ref):
    rank = inv_ref.shape[0]
    b = b_ref[:, :rank]
    gram_b = dot32(b, b, ((0,), (0,)), None)
    z = pairs_ref[...]
    twin = dot32(z, z, ((0,), (0,)), None)
    gram_c = twin[:rank, :rank] + twin[rank:, rank:]
    gram_b_ref[...] = gram_b
    inv_ref[...] = spd_inverse(gram_b * gram_c)


def keep_kernel(tiles_ref, kept_ref, sem):
    copy = pltpu.make_async_copy(tiles_ref.at[pl.ds(0, kept_ref.shape[0])], kept_ref, sem)
    copy.start()
    copy.wait()


def tile_copies(tiles_ref, late, sems):
    kept = tiles_ref.shape[0] - late.shape[0]
    copies = [pltpu.make_async_copy(tiles_ref.at[kept + t], late.at[t], sems.at[t]) for t in range(late.shape[0])]
    for copy in copies:
        copy.start()
    return [None] * kept + copies


def both_halves(kept_ref, late, t, start, size):
    kept, tile_i, tile_j, tile_k = kept_ref.shape
    tile, at = (kept_ref, t) if t < kept else (late, t - kept)
    upper = tile[at, start : start + size].reshape(size * tile_j, tile_k)
    lower = tile[at, tile_i // 2 + start : tile_i // 2 + start + size].reshape(size * tile_j, tile_k)
    return jnp.concatenate([upper, lower], axis=1)


def first_product_kernel(prov_ref, month_ref, tiles_ref, kept_ref, c_ref, b_ref, out_ref, late, sems):
    copies = tile_copies(tiles_ref, late, sems)
    out_ref[...] = jnp.zeros_like(out_ref)
    c = c_ref[...]
    zero = jnp.zeros_like(c)
    twice_c = jnp.concatenate([jnp.concatenate([c, zero], axis=1), jnp.concatenate([zero, c], axis=1)], axis=0)
    half, tile_j = tiles_ref.shape[1] // 2, tiles_ref.shape[2]
    size = half // 4
    for t, copy in enumerate(copies):
        if copy is not None:
            copy.wait()
        b = b_ref[month_ref[t]][None]
        for start in range(0, half, size):
            product = dot32(both_halves(kept_ref, late, t, start, size), twice_c, ((1,), (0,)), None)
            product = product.reshape(size, tile_j, -1) * b
            out_ref[prov_ref[t], start : start + size] += jnp.sum(product, axis=1)


def solve_kernel(got_ref, inv_ref, out_ref, own_ref):
    rank = inv_ref.shape[0]
    total = got_ref[0]
    for source in range(1, got_ref.shape[0]):
        total = total + got_ref[source]
    inv = inv_ref[...]
    upper = dot32(total[:, :rank], inv, ((1,), (0,)))
    lower = dot32(total[:, rank:], inv, ((1,), (0,)))
    solved = jnp.concatenate([upper, lower], axis=1)
    for target in range(out_ref.shape[0]):
        out_ref[target] = solved
    own_ref[: upper.shape[0]] = upper
    own_ref[upper.shape[0] :] = lower


def gram_kernel(a_ref, out_ref):
    rank = a_ref.shape[2] // 2
    rows = a_ref[...].reshape(-1, 2 * rank)
    twin = dot32(rows, rows, ((0,), (0,)))
    gram = twin[:rank, :rank] + twin[rank:, rank:]
    groups = out_ref.shape[0]
    for j in range(rank // groups):
        out_ref[:, j * rank : (j + 1) * rank] = gram[j * groups : (j + 1) * groups]


def last_product_kernel(at_ref, month_ref, tiles_ref, kept_ref, a_ref, other_ref, b_ref, out_ref, late, sems, turned):
    copies = tile_copies(tiles_ref, late, sems)
    blocks, half, lanes = a_ref.shape
    rank, tile_j, tile_k = lanes // 2, tiles_ref.shape[2], tiles_ref.shape[3]
    size = half // 4
    total = None
    for t, copy in enumerate(copies):
        if copy is not None:
            copy.wait()
        at = at_ref[t]
        b = b_ref[month_ref[t]][None]
        for start in range(0, half, size):
            rows = pl.ds(start, size)
            a = jnp.where(at < blocks, a_ref[at % blocks, rows], other_ref[at % blocks, rows])
            joint = (a[:, None, :] * b).reshape(size * tile_j, lanes).T
            high = joint.astype(jnp.bfloat16)
            low = (joint - high.astype(jnp.float32)).astype(jnp.bfloat16)
            both = jnp.concatenate([high, low], axis=0)
            part = dot32(both, both_halves(kept_ref, late, t, start, size), ((1,), (0,)), None)
            total = part if total is None else total + part
    parts = [total[k * rank : (k + 1) * rank, (k % 2) * tile_k : (k % 2 + 1) * tile_k] for k in range(4)]
    turned[...] = (parts[0] + parts[1] + parts[2] + parts[3]).T
    out_rows = lanes // rank
    for row in range(out_rows):
        out_ref[:, row * rank : (row + 1) * rank] = turned[pl.ds(row, tile_k // out_rows, stride=out_rows), :]


def last_kernel(got_ref, gram_b_ref, out_ref):
    rank = gram_b_ref.shape[0]
    width = got_ref.shape[1]
    lead = out_ref.shape[0] * rank
    groups = rank * rank // (width - lead)
    got = got_ref[...]
    rows = jnp.sum(got[:, :lead], axis=0, keepdims=True)
    own = jnp.concatenate([rows[:, j * rank : (j + 1) * rank] for j in range(out_ref.shape[0])], axis=0)
    n_zl = groups // 2
    per = got.shape[0] // n_zl
    folded = []
    for zl in range(n_zl):
        part = jnp.sum(got[zl * per : (zl + 1) * per, lead:].reshape(per // 8, 8, width - lead), axis=0)
        folded.append((part[0:2] + part[2:4]) + (part[4:6] + part[6:8]))
    folded = jnp.concatenate(folded, axis=0)
    gram = jnp.concatenate([folded[:, j * rank : (j + 1) * rank] for j in range(rank // groups)], axis=0)
    square_row, square_col = diagonals(gram)
    scale_row = jnp.sqrt(square_row + epsilon)
    scale_col = jnp.sqrt(square_col + epsilon)
    system = gram / scale_col / scale_row * gram_b_ref[...]
    out_ref[...] = dot32(own / scale_row, spd_inverse(system), ((1,), (0,)))


def shards(tile_values, prov_block, month_block, factor_b, factor_c):
    tiles, tile_i, tile_j, tile_k = tile_values.shape
    rank = factor_b.shape[1]
    n_prov = lax.axis_size(PROV)
    n_month = lax.axis_size("month")
    n_bin = lax.axis_size(BIN)
    month = lax.axis_index("month")
    bin_at = lax.axis_index(BIN)

    n_all = n_prov * n_month * n_bin
    c_rows = factor_c.shape[0] // n_month
    b_rep = n_bin // factor_b.shape[0]
    own_c_rows = lax.dynamic_slice_in_dim(factor_c, month * c_rows, c_rows, 0).reshape(1, c_rows * rank)
    own_b_row = lax.dynamic_slice_in_dim(factor_b, bin_at // b_rep, 1, 0)
    own_b_row = jnp.concatenate([own_b_row] * c_rows, axis=1)
    chunk = jnp.concatenate([own_c_rows, own_b_row], axis=0)
    sent = jnp.broadcast_to(chunk[None], (n_all,) + chunk.shape)
    got = lax.all_to_all(sent, PROV + BIN + ("month",), 0, 0, tiled=True)
    pairs_c = got[:, 0, :]
    twice_b = got[:, 1, :].reshape(n_prov, factor_b.shape[0], b_rep, n_month, c_rows * rank)[:, :, 0]
    twice_b = twice_b.transpose(0, 2, 1, 3).reshape(-1, c_rows * rank)

    slab_pairs = lax.dynamic_slice_in_dim(pairs_c, bin_at * (tile_k // c_rows), tile_k // c_rows, 0)
    slab_c = slab_pairs.reshape(tile_k, rank)
    slab_b = lax.dynamic_slice_in_dim(twice_b, month * (MB_DEV * tile_j), MB_DEV * tile_j, 0)
    slab_b = slab_b.astype(jnp.float32).reshape(MB_DEV, tile_j, c_rows * rank)

    smem, vmem, hbm = (pl.BlockSpec(memory_space=space) for space in (pltpu.SMEM, pltpu.VMEM, pl.ANY))
    kept = pl.pallas_call(
        keep_kernel,
        out_shape=jax.ShapeDtypeStruct((KEPT,) + tile_values.shape[1:], tile_values.dtype),
        in_specs=[hbm],
        out_specs=vmem,
        scratch_shapes=[pltpu.SemaphoreType.DMA],
        compiler_params=LARGE,
        name="keep_tiles",
    )(tile_values)
    late = tiles - KEPT
    tile_scratch = [
        pltpu.VMEM((late,) + tile_values.shape[1:], tile_values.dtype),
        pltpu.SemaphoreType.DMA((late,)),
    ]
    half = tile_i // 2
    prov_at = jnp.clip(prov_block, 0, PB_DEV - 1)
    month_at = jnp.clip(month_block, 0, MB_DEV - 1)
    partial_a = pl.pallas_call(
        first_product_kernel,
        out_shape=jax.ShapeDtypeStruct((PB_DEV, half, 2 * rank), jnp.float32),
        in_specs=[smem, smem, hbm, vmem, vmem, vmem],
        out_specs=vmem,
        scratch_shapes=tile_scratch,
        compiler_params=LARGE,
        name="first_product",
    )(prov_at, month_at, tile_values, kept, slab_c, slab_b)

    pair_a = lax.all_to_all(partial_a.reshape(n_month, n_bin, half, 2 * rank), "month", 0, 0, tiled=True)
    pair_a = jnp.sum(pair_a, axis=0)
    twice_b, pairs_c, pair_a = lax.optimization_barrier((twice_b, pairs_c, pair_a))
    own_a = lax.all_to_all(pair_a, BIN, 0, 0, tiled=True)

    square = jax.ShapeDtypeStruct((rank, rank), jnp.float32)
    inverse, gram_b = pl.pallas_call(
        first_inverse_kernel,
        out_shape=(square, square),
        cost_estimate=pl.CostEstimate(flops=20000000, bytes_accessed=200000, transcendentals=0),
        name="first_inverse",
        compiler_params=SMALL,
    )(twice_b, pairs_c)
    spread, factor_a = pl.pallas_call(
        solve_kernel,
        out_shape=(
            jax.ShapeDtypeStruct(own_a.shape, jnp.float32),
            jax.ShapeDtypeStruct((tile_i, rank), jnp.float32),
        ),
        compiler_params=SMALL,
        name="solve_first",
    )(own_a, inverse)

    half_a = lax.all_to_all(spread, BIN, 0, 0, tiled=True)
    n_gram = lax.axis_size(GRAM)
    half_gram = pl.pallas_call(
        gram_kernel,
        out_shape=jax.ShapeDtypeStruct((n_gram, rank * rank // n_gram), jnp.float32),
        compiler_params=SMALL,
        name="half_gram",
    )(half_a)
    gram_rows = lax.all_to_all(half_gram[:, None, :], GRAM, 0, 0, tiled=True)

    other_a = lax.ppermute(half_a, "month", [(i, n_month - 1 - i) for i in range(n_month)])

    n_out = n_prov * n_month
    out_rows = tile_k // n_out
    partial_c = pl.pallas_call(
        last_product_kernel,
        out_shape=jax.ShapeDtypeStruct((n_out, out_rows * rank), jnp.float32),
        in_specs=[smem, smem, hbm, vmem, vmem, vmem, vmem],
        out_specs=vmem,
        scratch_shapes=tile_scratch + [pltpu.VMEM((tile_k, rank), jnp.float32)],
        compiler_params=LARGE,
        name="last_product",
    )(prov_at ^ (month * n_bin), month_at, tile_values, kept, half_a, other_a, slab_b)

    gram_rows, partial_c = lax.optimization_barrier((gram_rows, partial_c))
    gram_row = jnp.sum(gram_rows, axis=0, keepdims=True)
    sent_row = jnp.broadcast_to(gram_row, (n_out,) + gram_row.shape[1:])
    last = jnp.concatenate([partial_c[:, None, :], sent_row], axis=2)
    last = lax.all_to_all(last, PROV + ("month",), 0, 0, tiled=True)
    new_c = pl.pallas_call(
        last_kernel,
        out_shape=jax.ShapeDtypeStruct((out_rows, rank), jnp.float32),
        compiler_params=SMALL,
        name="last_solve",
    )(last.reshape(n_out, -1), gram_b)
    return (factor_a, new_c)


def solution(mesh):
    prov, month, bins = mesh.devices.shape
    shape = (prov // 8, 8, month, bins // 2, 2)
    mesh = jax.sharding.Mesh(mesh.devices.reshape(shape), ("zl", "y", "month", "x", "zh"))
    everywhere = PROV + ("month",) + BIN
    in_specs = (
        P(everywhere, None, None, None),
        P(everywhere),
        P(everywhere),
        P(PROV + ("month",), None),
        P(PROV + BIN, None),
    )
    out_specs = (P(everywhere, None), P(BIN + PROV + ("month",), None))
    return jax.shard_map(shards, mesh=mesh, in_specs=in_specs, out_specs=out_specs, check_vma=False)
```

```python
import jax
import jax.numpy as jnp
from jax import lax
from jax.experimental import pallas as pl
from jax.experimental.pallas import tpu as pltpu
from jax.sharding import PartitionSpec as P

MB_DEV = 8
KEPT = 5
PB_DEV = 16
epsilon = 1e-06
HIGH = lax.Precision.HIGHEST
SMALL = pltpu.CompilerParams(vmem_limit_bytes=8 * 1024 * 1024)
LARGE = pltpu.CompilerParams(vmem_limit_bytes=50 * 1024 * 1024)
PROV = ("zl", "y")
BIN = ("x", "zh")


def dot32(a, b, dims, precision=HIGH):
    return lax.dot_general(a, b, (dims, ((), ())), precision=precision, preferred_element_type=jnp.float32)


def diagonals(a):
    lane = lax.broadcasted_iota(jnp.int32, a.shape, 1)
    sub = lax.broadcasted_iota(jnp.int32, a.shape, 0)
    diag = jnp.where(lane == sub, a, 0.0)
    return jnp.sum(diag, axis=0, keepdims=True), jnp.sum(diag, axis=1, keepdims=True)


def spd_inverse(a):
    n = a.shape[0]
    in_row, in_col = diagonals(a)
    in_row, in_col = lax.rsqrt(in_row), lax.rsqrt(in_col)
    a = a * in_col * in_row
    lane = lax.broadcasted_iota(jnp.int32, a.shape, 1)
    sub = lax.broadcasted_iota(jnp.int32, a.shape, 0)
    lane_row = lax.broadcasted_iota(jnp.int32, (1, n), 1)
    for k in range(0, n, 2):
        col0 = jnp.broadcast_to(a[:, k : k + 1], a.shape)
        col1 = jnp.broadcast_to(a[:, k + 1 : k + 2], a.shape)
        p, q, s = col0[k : k + 1], col1[k : k + 1], col1[k + 1 : k + 2]
        inv = 1.0 / (p * s - q * q)
        p, q, s = p * inv, q * inv, s * inv
        row0, row1 = a[k : k + 1], a[k + 1 : k + 2]
        first, second = lane_row == k, lane_row == k + 1
        new0 = jnp.where(first, s, jnp.where(second, -q, s * row0 - q * row1))
        new1 = jnp.where(first, -q, jnp.where(second, p, p * row1 - q * row0))
        rest = jnp.where((lane == k) | (lane == k + 1), 0.0, a) - col0 * new0 - col1 * new1
        a = jnp.where(sub == k, new0, jnp.where(sub == k + 1, new1, rest))
    return a * in_col * in_row


def first_inverse_kernel(b_ref, pairs_ref, inv_ref, gram_b_ref):
    rank = inv_ref.shape[0]
    b = b_ref[:, :rank]
    gram_b = dot32(b, b, ((0,), (0,)), None)
    z = pairs_ref[...]
    twin = dot32(z, z, ((0,), (0,)), None)
    gram_c = twin[:rank, :rank] + twin[rank:, rank:]
    gram_b_ref[...] = gram_b
    inv_ref[...] = spd_inverse(gram_b * gram_c)


def keep_kernel(tiles_ref, kept_ref, sem):
    copy = pltpu.make_async_copy(tiles_ref.at[pl.ds(0, kept_ref.shape[0])], kept_ref, sem)
    copy.start()
    copy.wait()


def tile_copies(tiles_ref, late, sems):
    kept = tiles_ref.shape[0] - late.shape[0]
    copies = [pltpu.make_async_copy(tiles_ref.at[kept + t], late.at[t], sems.at[t]) for t in range(late.shape[0])]
    for copy in copies:
        copy.start()
    return [None] * kept + copies


def both_halves(kept_ref, late, t, start, size):
    kept, tile_i, tile_j, tile_k = kept_ref.shape
    tile, at = (kept_ref, t) if t < kept else (late, t - kept)
    upper = tile[at, start : start + size].reshape(size * tile_j, tile_k)
    lower = tile[at, tile_i // 2 + start : tile_i // 2 + start + size].reshape(size * tile_j, tile_k)
    return jnp.concatenate([upper, lower], axis=1)


def first_product_kernel(prov_ref, month_ref, tiles_ref, kept_ref, c_ref, b_ref, out_ref, late, sems):
    copies = tile_copies(tiles_ref, late, sems)
    out_ref[...] = jnp.zeros_like(out_ref)
    c = c_ref[...]
    zero = jnp.zeros_like(c)
    twice_c = jnp.concatenate([jnp.concatenate([c, zero], axis=1), jnp.concatenate([zero, c], axis=1)], axis=0)
    half, tile_j = tiles_ref.shape[1] // 2, tiles_ref.shape[2]
    size = half // 4
    for t, copy in enumerate(copies):
        if copy is not None:
            copy.wait()
        b = b_ref[month_ref[t]][None]
        for start in range(0, half, size):
            product = dot32(both_halves(kept_ref, late, t, start, size), twice_c, ((1,), (0,)), None)
            product = product.reshape(size, tile_j, -1) * b
            out_ref[prov_ref[t], start : start + size] += jnp.sum(product, axis=1)


def solve_kernel(got_ref, inv_ref, out_ref, own_ref):
    rank = inv_ref.shape[0]
    total = got_ref[0]
    for source in range(1, got_ref.shape[0]):
        total = total + got_ref[source]
    inv = inv_ref[...]
    upper = dot32(total[:, :rank], inv, ((1,), (0,)))
    lower = dot32(total[:, rank:], inv, ((1,), (0,)))
    solved = jnp.concatenate([upper, lower], axis=1)
    for target in range(out_ref.shape[0]):
        out_ref[target] = solved
    own_ref[: upper.shape[0]] = upper
    own_ref[upper.shape[0] :] = lower


def iotas(n):
    return lax.broadcasted_iota(jnp.int32, (n, n), 0), lax.broadcasted_iota(jnp.int32, (n, n), 1)


def pack_gram(gram, month):
    n = gram.shape[0] // 2
    row, column = iotas(n)
    last = gram[n:, n:]
    triangles = jnp.where(row >= column, gram[:n, :n], last)
    mine = jnp.where(month == 0, gram[:n, n:], triangles)
    per = n // 4
    folded = jnp.concatenate([mine[k * per : (k + 1) * per] for k in range(4)], axis=1)
    diagonal = jnp.sum(jnp.where(row == column, last, 0.0), axis=0, keepdims=True)
    return folded, jnp.concatenate([diagonal, jnp.zeros((1, 3 * n), jnp.float32)], axis=1)


def unpack_gram(block, triangles, diagonal):
    n = diagonal.shape[1]
    row, column = iotas(n)

    def square(flat):
        rows = jnp.concatenate([flat[:, k * 4 * n : (k + 1) * 4 * n] for k in range(n // 4)], axis=0)
        return jnp.concatenate([rows[:, k * n : (k + 1) * n] for k in range(4)], axis=0)

    block, triangles = square(block), square(triangles)
    turned = triangles.T
    first = jnp.where(row >= column, triangles, turned)
    last = jnp.where(row < column, triangles, jnp.where(row > column, turned, diagonal))
    return jnp.concatenate(
        [jnp.concatenate([first, block], axis=1), jnp.concatenate([block.T, last], axis=1)], axis=0
    )


def last_product_kernel(at_ref, month_ref, tiles_ref, kept_ref, a_ref, other_ref, b_ref, out_ref, gram_ref, late, sems, turned):
    copies = tile_copies(tiles_ref, late, sems)
    blocks, half, lanes = a_ref.shape
    rank, tile_j, tile_k = lanes // 2, tiles_ref.shape[2], tiles_ref.shape[3]
    size = half // 4
    own, other = (ref[...].reshape(blocks * half, lanes) for ref in (a_ref, other_ref))
    twin = dot32(own, own, ((0,), (0,))) + dot32(other, other, ((0,), (0,)))
    folded, diagonal = pack_gram(twin[:rank, :rank] + twin[rank:, rank:], month_ref[month_ref.shape[0] - 1])
    gram_ref[: folded.shape[0]] = folded
    gram_ref[folded.shape[0] :] = diagonal
    total = None
    for t, copy in enumerate(copies):
        if copy is not None:
            copy.wait()
        at = at_ref[t]
        b = b_ref[month_ref[t]][None]
        for start in range(0, half, size):
            rows = pl.ds(start, size)
            a = jnp.where(at < blocks, a_ref[at % blocks, rows], other_ref[at % blocks, rows])
            joint = (a[:, None, :] * b).reshape(size * tile_j, lanes).T
            high = joint.astype(jnp.bfloat16)
            low = (joint - high.astype(jnp.float32)).astype(jnp.bfloat16)
            both = jnp.concatenate([high, low], axis=0)
            part = dot32(both, both_halves(kept_ref, late, t, start, size), ((1,), (0,)), None)
            total = part if total is None else total + part
    parts = [total[k * rank : (k + 1) * rank, (k % 2) * tile_k : (k % 2 + 1) * tile_k] for k in range(4)]
    turned[...] = (parts[0] + parts[1] + parts[2] + parts[3]).T
    out_rows = lanes // rank
    for row in range(out_rows):
        out_ref[:, row * rank : (row + 1) * rank] = turned[pl.ds(row, tile_k // out_rows, stride=out_rows), :]


def last_kernel(got_ref, gram_b_ref, out_ref):
    rank = gram_b_ref.shape[0]
    width = got_ref.shape[1]
    lead = out_ref.shape[0] * rank
    got = got_ref[...]
    total = jnp.sum(got.reshape(got.shape[0] // 8, 8, width), axis=0)
    total = (total[0:2] + total[2:4]) + (total[4:6] + total[6:8])
    rows = total[0:1, :lead] + total[1:2, :lead]
    own = jnp.concatenate([rows[:, j * rank : (j + 1) * rank] for j in range(out_ref.shape[0])], axis=0)
    end = lead + rank * rank // 4
    gram = unpack_gram(total[0:1, lead:end], total[1:2, lead:end], total[1:2, end : end + rank // 2])
    square_row, square_col = diagonals(gram)
    scale_row = jnp.sqrt(square_row + epsilon)
    scale_col = jnp.sqrt(square_col + epsilon)
    system = gram / scale_col / scale_row * gram_b_ref[...]
    out_ref[...] = dot32(own / scale_row, spd_inverse(system), ((1,), (0,)))


def shards(tile_values, prov_block, month_block, factor_b, factor_c):
    tiles, tile_i, tile_j, tile_k = tile_values.shape
    rank = factor_b.shape[1]
    n_prov = lax.axis_size(PROV)
    n_month = lax.axis_size("month")
    n_bin = lax.axis_size(BIN)
    month = lax.axis_index("month")
    bin_at = lax.axis_index(BIN)

    n_all = n_prov * n_month * n_bin
    c_rows = factor_c.shape[0] // n_month
    b_rep = n_bin // factor_b.shape[0]
    own_c_rows = lax.dynamic_slice_in_dim(factor_c, month * c_rows, c_rows, 0).reshape(1, c_rows * rank)
    own_b_row = lax.dynamic_slice_in_dim(factor_b, bin_at // b_rep, 1, 0)
    own_b_row = jnp.concatenate([own_b_row] * c_rows, axis=1)
    chunk = jnp.concatenate([own_c_rows, own_b_row], axis=0)
    sent = jnp.broadcast_to(chunk[None], (n_all,) + chunk.shape)
    got = lax.all_to_all(sent, PROV + BIN + ("month",), 0, 0, tiled=True)
    pairs_c = got[:, 0, :]
    twice_b = got[:, 1, :].reshape(n_prov, factor_b.shape[0], b_rep, n_month, c_rows * rank)[:, :, 0]
    twice_b = twice_b.transpose(0, 2, 1, 3).reshape(-1, c_rows * rank)

    slab_pairs = lax.dynamic_slice_in_dim(pairs_c, bin_at * (tile_k // c_rows), tile_k // c_rows, 0)
    slab_c = slab_pairs.reshape(tile_k, rank)
    slab_b = lax.dynamic_slice_in_dim(twice_b, month * (MB_DEV * tile_j), MB_DEV * tile_j, 0)
    slab_b = slab_b.astype(jnp.float32).reshape(MB_DEV, tile_j, c_rows * rank)

    smem, vmem, hbm = (pl.BlockSpec(memory_space=space) for space in (pltpu.SMEM, pltpu.VMEM, pl.ANY))
    kept = pl.pallas_call(
        keep_kernel,
        out_shape=jax.ShapeDtypeStruct((KEPT,) + tile_values.shape[1:], tile_values.dtype),
        in_specs=[hbm],
        out_specs=vmem,
        scratch_shapes=[pltpu.SemaphoreType.DMA],
        compiler_params=LARGE,
        name="keep_tiles",
    )(tile_values)
    late = tiles - KEPT
    tile_scratch = [
        pltpu.VMEM((late,) + tile_values.shape[1:], tile_values.dtype),
        pltpu.SemaphoreType.DMA((late,)),
    ]
    half = tile_i // 2
    prov_at = jnp.clip(prov_block, 0, PB_DEV - 1)
    month_at = jnp.clip(jnp.concatenate([month_block, month[None]]), 0, MB_DEV - 1)
    partial_a = pl.pallas_call(
        first_product_kernel,
        out_shape=jax.ShapeDtypeStruct((PB_DEV, half, 2 * rank), jnp.float32),
        in_specs=[smem, smem, hbm, vmem, vmem, vmem],
        out_specs=vmem,
        scratch_shapes=tile_scratch,
        compiler_params=LARGE,
        name="first_product",
    )(prov_at, month_at, tile_values, kept, slab_c, slab_b)

    pair_a = lax.all_to_all(partial_a.reshape(n_month, n_bin, half, 2 * rank), "month", 0, 0, tiled=True)
    pair_a = jnp.sum(pair_a, axis=0)
    twice_b, pairs_c, pair_a = lax.optimization_barrier((twice_b, pairs_c, pair_a))
    own_a = lax.all_to_all(pair_a, BIN, 0, 0, tiled=True)

    square = jax.ShapeDtypeStruct((rank, rank), jnp.float32)
    inverse, gram_b = pl.pallas_call(
        first_inverse_kernel,
        out_shape=(square, square),
        cost_estimate=pl.CostEstimate(flops=20000000, bytes_accessed=200000, transcendentals=0),
        name="first_inverse",
        compiler_params=SMALL,
    )(twice_b, pairs_c)
    spread, factor_a = pl.pallas_call(
        solve_kernel,
        out_shape=(
            jax.ShapeDtypeStruct(own_a.shape, jnp.float32),
            jax.ShapeDtypeStruct((tile_i, rank), jnp.float32),
        ),
        compiler_params=SMALL,
        name="solve_first",
    )(own_a, inverse)

    half_a = lax.all_to_all(spread, BIN, 0, 0, tiled=True)
    other_a = lax.ppermute(half_a, "month", [(i, n_month - 1 - i) for i in range(n_month)])

    n_out = n_prov * n_month
    out_rows = tile_k // n_out
    partial_c, packed = pl.pallas_call(
        last_product_kernel,
        out_shape=(
            jax.ShapeDtypeStruct((n_out, out_rows * rank), jnp.float32),
            jax.ShapeDtypeStruct((rank // 8 + 1, 2 * rank), jnp.float32),
        ),
        in_specs=[smem, smem, hbm, vmem, vmem, vmem, vmem],
        out_specs=(vmem, vmem),
        scratch_shapes=tile_scratch + [pltpu.VMEM((tile_k, rank), jnp.float32)],
        compiler_params=LARGE,
        name="last_product",
    )(prov_at ^ (month * n_bin), month_at, tile_values, kept, half_a, other_a, slab_b)

    sent_gram = jnp.broadcast_to(packed.reshape(1, 1, -1), (n_out, 1, packed.size))
    last = jnp.concatenate([partial_c[:, None, :], sent_gram], axis=2)
    last = lax.all_to_all(last, PROV + ("month",), 0, 0, tiled=True)
    new_c = pl.pallas_call(
        last_kernel,
        out_shape=jax.ShapeDtypeStruct((out_rows, rank), jnp.float32),
        compiler_params=SMALL,
        name="last_solve",
    )(last.reshape(n_out, -1), gram_b)
    return (factor_a, new_c)


def solution(mesh):
    prov, month, bins = mesh.devices.shape
    shape = (prov // 8, 8, month, bins // 2, 2)
    mesh = jax.sharding.Mesh(mesh.devices.reshape(shape), ("zl", "y", "month", "x", "zh"))
    everywhere = PROV + ("month",) + BIN
    in_specs = (
        P(everywhere, None, None, None),
        P(everywhere),
        P(everywhere),
        P(PROV + ("month",), None),
        P(PROV + BIN, None),
    )
    out_specs = (P(everywhere, None), P(BIN + PROV + ("month",), None))
    return jax.shard_map(shards, mesh=mesh, in_specs=in_specs, out_specs=out_specs, check_vma=False)
```

```python
import jax
import jax.numpy as jnp
from jax import lax
from jax.experimental import pallas as pl
from jax.experimental.pallas import tpu as pltpu
from jax.sharding import PartitionSpec as P

MB_DEV = 8
KEPT = 5
PB_DEV = 16
epsilon = 1e-06
HIGH = lax.Precision.HIGHEST
SMALL = pltpu.CompilerParams(vmem_limit_bytes=8 * 1024 * 1024)
LARGE = pltpu.CompilerParams(vmem_limit_bytes=50 * 1024 * 1024)
PROV = ("zl", "y")
BIN = ("x", "zh")


def dot32(a, b, dims, precision=HIGH):
    return lax.dot_general(a, b, (dims, ((), ())), precision=precision, preferred_element_type=jnp.float32)


def diagonals(a):
    lane = lax.broadcasted_iota(jnp.int32, a.shape, 1)
    sub = lax.broadcasted_iota(jnp.int32, a.shape, 0)
    diag = jnp.where(lane == sub, a, 0.0)
    return jnp.sum(diag, axis=0, keepdims=True), jnp.sum(diag, axis=1, keepdims=True)


def spd_inverse(a):
    n = a.shape[0]
    in_row, in_col = diagonals(a)
    in_row, in_col = lax.rsqrt(in_row), lax.rsqrt(in_col)
    a = a * in_col * in_row
    lane = lax.broadcasted_iota(jnp.int32, a.shape, 1)
    sub = lax.broadcasted_iota(jnp.int32, a.shape, 0)
    lane_row = lax.broadcasted_iota(jnp.int32, (1, n), 1)
    for k in range(0, n, 4):
        cols = [jnp.broadcast_to(a[:, k + j : k + j + 1], a.shape) for j in range(4)]
        (p00, p01, p02, p03), (_, p11, p12, p13), (_, _, p22, p23), (_, _, _, p33) = [
            [cols[j][k + i : k + i + 1] for j in range(4)] for i in range(4)
        ]
        inv = 1.0 / (p00 * p11 - p01 * p01)
        e00, e01, e11 = p11 * inv, -p01 * inv, p00 * inv
        w00, w01 = e00 * p02 + e01 * p12, e00 * p03 + e01 * p13
        w10, w11 = e01 * p02 + e11 * p12, e01 * p03 + e11 * p13
        s00, s01 = p22 - (p02 * w00 + p12 * w10), p23 - (p02 * w01 + p12 * w11)
        s11 = p33 - (p03 * w01 + p13 * w11)
        inv = 1.0 / (s00 * s11 - s01 * s01)
        q22, q23, q33 = s11 * inv, -s01 * inv, s00 * inv
        v00, v01 = w00 * q22 + w01 * q23, w00 * q23 + w01 * q33
        v10, v11 = w10 * q22 + w11 * q23, w10 * q23 + w11 * q33
        q01 = e01 + v00 * w10 + v01 * w11
        pivot = (
            (e00 + v00 * w00 + v01 * w01, q01, -v00, -v01),
            (q01, e11 + v10 * w10 + v11 * w11, -v10, -v11),
            (-v00, -v10, q22, q23),
            (-v01, -v11, q23, q33),
        )
        rows = [a[k + j : k + j + 1] for j in range(4)]
        rest = jnp.where((lane >= k) & (lane < k + 4), 0.0, a)
        fresh = []
        for i in range(4):
            q = pivot[i]
            new = (q[0] * rows[0] + q[1] * rows[1]) + (q[2] * rows[2] + q[3] * rows[3])
            for j in range(4):
                new = jnp.where(lane_row == k + j, q[j], new)
            fresh.append(new)
        a = rest - ((cols[0] * fresh[0] + cols[1] * fresh[1]) + (cols[2] * fresh[2] + cols[3] * fresh[3]))
        for i in range(4):
            a = jnp.where(sub == k + i, fresh[i], a)
    return a * in_col * in_row


def first_inverse_kernel(b_ref, pairs_ref, inv_ref, gram_b_ref):
    rank = inv_ref.shape[0]
    b = b_ref[:, :rank]
    gram_b = dot32(b, b, ((0,), (0,)), None)
    z = pairs_ref[...]
    twin = dot32(z, z, ((0,), (0,)), None)
    gram_c = twin[:rank, :rank] + twin[rank:, rank:]
    gram_b_ref[...] = gram_b
    inv_ref[...] = spd_inverse(gram_b * gram_c)


def keep_kernel(tiles_ref, kept_ref, sem):
    copy = pltpu.make_async_copy(tiles_ref.at[pl.ds(0, kept_ref.shape[0])], kept_ref, sem)
    copy.start()
    copy.wait()


def tile_copies(tiles_ref, late, sems):
    kept = tiles_ref.shape[0] - late.shape[0]
    copies = [pltpu.make_async_copy(tiles_ref.at[kept + t], late.at[t], sems.at[t]) for t in range(late.shape[0])]
    for copy in copies:
        copy.start()
    return [None] * kept + copies


def both_halves(kept_ref, late, t, start, size):
    kept, tile_i, tile_j, tile_k = kept_ref.shape
    tile, at = (kept_ref, t) if t < kept else (late, t - kept)
    upper = tile[at, start : start + size].reshape(size * tile_j, tile_k)
    lower = tile[at, tile_i // 2 + start : tile_i // 2 + start + size].reshape(size * tile_j, tile_k)
    return jnp.concatenate([upper, lower], axis=1)


def first_product_kernel(at_ref, month_ref, tiles_ref, kept_ref, c_ref, b_ref, own_ref, other_ref, late, sems):
    copies = tile_copies(tiles_ref, late, sems)
    own_ref[...] = jnp.zeros_like(own_ref)
    other_ref[...] = jnp.zeros_like(other_ref)
    c = c_ref[...]
    blocks = own_ref.shape[0]
    zero = jnp.zeros_like(c)
    twice_c = jnp.concatenate([jnp.concatenate([c, zero], axis=1), jnp.concatenate([zero, c], axis=1)], axis=0)
    half, tile_j = tiles_ref.shape[1] // 2, tiles_ref.shape[2]
    size = half // 4
    for t, copy in enumerate(copies):
        if copy is not None:
            copy.wait()
        at = at_ref[t]
        b = b_ref[month_ref[t]][None]
        for start in range(0, half, size):
            product = dot32(both_halves(kept_ref, late, t, start, size), twice_c, ((1,), (0,)), None)
            product = product.reshape(size, tile_j, -1) * b
            product = jnp.sum(product, axis=1)
            rows = pl.ds(start, size)
            own_ref[at % blocks, rows] += jnp.where(at < blocks, product, 0.0)
            other_ref[at % blocks, rows] += jnp.where(at < blocks, 0.0, product)


def solve_kernel(got_ref, inv_ref, out_ref, own_ref):
    rank = inv_ref.shape[0]
    total = got_ref[0]
    for source in range(1, got_ref.shape[0]):
        total = total + got_ref[source]
    inv = inv_ref[...]
    upper = dot32(total[:, :rank], inv, ((1,), (0,)))
    lower = dot32(total[:, rank:], inv, ((1,), (0,)))
    solved = jnp.concatenate([upper, lower], axis=1)
    for target in range(out_ref.shape[0]):
        out_ref[target] = solved
    own_ref[: upper.shape[0]] = upper
    own_ref[upper.shape[0] :] = lower


def iotas(n):
    return lax.broadcasted_iota(jnp.int32, (n, n), 0), lax.broadcasted_iota(jnp.int32, (n, n), 1)


def pack_gram(gram, month):
    n = gram.shape[0] // 2
    row, column = iotas(n)
    last = gram[n:, n:]
    triangles = jnp.where(row >= column, gram[:n, :n], last)
    mine = jnp.where(month == 0, gram[:n, n:], triangles)
    per = n // 4
    folded = jnp.concatenate([mine[k * per : (k + 1) * per] for k in range(4)], axis=1)
    diagonal = jnp.sum(jnp.where(row == column, last, 0.0), axis=0, keepdims=True)
    return folded, jnp.concatenate([diagonal, jnp.zeros((1, 3 * n), jnp.float32)], axis=1)


def unpack_gram(block, triangles, diagonal):
    n = diagonal.shape[1]
    row, column = iotas(n)

    def square(flat):
        rows = jnp.concatenate([flat[:, k * 4 * n : (k + 1) * 4 * n] for k in range(n // 4)], axis=0)
        return jnp.concatenate([rows[:, k * n : (k + 1) * n] for k in range(4)], axis=0)

    block, triangles = square(block), square(triangles)
    turned = triangles.T
    first = jnp.where(row >= column, triangles, turned)
    last = jnp.where(row < column, triangles, jnp.where(row > column, turned, diagonal))
    return jnp.concatenate(
        [jnp.concatenate([first, block], axis=1), jnp.concatenate([block.T, last], axis=1)], axis=0
    )


def last_product_kernel(at_ref, month_ref, tiles_ref, kept_ref, a_ref, other_ref, b_ref, out_ref, gram_ref, late, sems, turned):
    copies = tile_copies(tiles_ref, late, sems)
    blocks, half, lanes = a_ref.shape
    rank, tile_j, tile_k = lanes // 2, tiles_ref.shape[2], tiles_ref.shape[3]
    size = half // 4
    own, other = (ref[...].reshape(blocks * half, lanes) for ref in (a_ref, other_ref))
    twin = dot32(own, own, ((0,), (0,))) + dot32(other, other, ((0,), (0,)))
    folded, diagonal = pack_gram(twin[:rank, :rank] + twin[rank:, rank:], month_ref[month_ref.shape[0] - 1])
    gram_ref[: folded.shape[0]] = folded
    gram_ref[folded.shape[0] :] = diagonal
    total = None
    for t, copy in enumerate(copies):
        if copy is not None:
            copy.wait()
        at = at_ref[t]
        b = b_ref[month_ref[t]][None]
        for start in range(0, half, size):
            rows = pl.ds(start, size)
            a = jnp.where(at < blocks, a_ref[at % blocks, rows], other_ref[at % blocks, rows])
            joint = (a[:, None, :] * b).reshape(size * tile_j, lanes).T
            high = joint.astype(jnp.bfloat16)
            low = (joint - high.astype(jnp.float32)).astype(jnp.bfloat16)
            both = jnp.concatenate([high, low], axis=0)
            part = dot32(both, both_halves(kept_ref, late, t, start, size), ((1,), (0,)), None)
            total = part if total is None else total + part
    parts = [total[k * rank : (k + 1) * rank, (k % 2) * tile_k : (k % 2 + 1) * tile_k] for k in range(4)]
    turned[...] = (parts[0] + parts[1] + parts[2] + parts[3]).T
    out_rows = lanes // rank
    for row in range(out_rows):
        out_ref[:, row * rank : (row + 1) * rank] = turned[pl.ds(row, tile_k // out_rows, stride=out_rows), :]


def last_kernel(got_ref, gram_b_ref, out_ref):
    rank = gram_b_ref.shape[0]
    width = got_ref.shape[1]
    lead = out_ref.shape[0] * rank
    got = got_ref[...]
    total = jnp.sum(got.reshape(got.shape[0] // 8, 8, width), axis=0)
    total = (total[0:2] + total[2:4]) + (total[4:6] + total[6:8])
    rows = total[0:1, :lead] + total[1:2, :lead]
    own = jnp.concatenate([rows[:, j * rank : (j + 1) * rank] for j in range(out_ref.shape[0])], axis=0)
    end = lead + rank * rank // 4
    gram = unpack_gram(total[0:1, lead:end], total[1:2, lead:end], total[1:2, end : end + rank // 2])
    square_row, square_col = diagonals(gram)
    scale_row = jnp.sqrt(square_row + epsilon)
    scale_col = jnp.sqrt(square_col + epsilon)
    system = gram / scale_col / scale_row * gram_b_ref[...]
    out_ref[...] = dot32(own / scale_row, spd_inverse(system), ((1,), (0,)))


def shards(tile_values, prov_block, month_block, factor_b, factor_c):
    tiles, tile_i, tile_j, tile_k = tile_values.shape
    rank = factor_b.shape[1]
    n_prov = lax.axis_size(PROV)
    n_month = lax.axis_size("month")
    n_bin = lax.axis_size(BIN)
    month = lax.axis_index("month")
    bin_at = lax.axis_index(BIN)

    n_all = n_prov * n_month * n_bin
    c_rows = factor_c.shape[0] // n_month
    b_rep = n_bin // factor_b.shape[0]
    own_c_rows = lax.dynamic_slice_in_dim(factor_c, month * c_rows, c_rows, 0).reshape(1, c_rows * rank)
    own_b_row = lax.dynamic_slice_in_dim(factor_b, bin_at // b_rep, 1, 0)
    own_b_row = jnp.concatenate([own_b_row] * c_rows, axis=1)
    chunk = jnp.concatenate([own_c_rows, own_b_row], axis=0)
    sent = jnp.broadcast_to(chunk[None], (n_all,) + chunk.shape)
    got = lax.all_to_all(sent, PROV + BIN + ("month",), 0, 0, tiled=True)
    pairs_c = got[:, 0, :]
    twice_b = got[:, 1, :].reshape(n_prov, factor_b.shape[0], b_rep, n_month, c_rows * rank)[:, :, 0]
    twice_b = twice_b.transpose(0, 2, 1, 3).reshape(-1, c_rows * rank)

    slab_pairs = lax.dynamic_slice_in_dim(pairs_c, bin_at * (tile_k // c_rows), tile_k // c_rows, 0)
    slab_c = slab_pairs.reshape(tile_k, rank)
    slab_b = lax.dynamic_slice_in_dim(twice_b, month * (MB_DEV * tile_j), MB_DEV * tile_j, 0)
    slab_b = slab_b.astype(jnp.float32).reshape(MB_DEV, tile_j, c_rows * rank)

    smem, vmem, hbm = (pl.BlockSpec(memory_space=space) for space in (pltpu.SMEM, pltpu.VMEM, pl.ANY))
    kept = pl.pallas_call(
        keep_kernel,
        out_shape=jax.ShapeDtypeStruct((KEPT,) + tile_values.shape[1:], tile_values.dtype),
        in_specs=[hbm],
        out_specs=vmem,
        scratch_shapes=[pltpu.SemaphoreType.DMA],
        compiler_params=LARGE,
        name="keep_tiles",
    )(tile_values)
    late = tiles - KEPT
    tile_scratch = [
        pltpu.VMEM((late,) + tile_values.shape[1:], tile_values.dtype),
        pltpu.SemaphoreType.DMA((late,)),
    ]
    half = tile_i // 2
    prov_at = jnp.clip(prov_block, 0, PB_DEV - 1)
    month_at = jnp.clip(jnp.concatenate([month_block, month[None]]), 0, MB_DEV - 1)
    swap = [(i, n_month - 1 - i) for i in range(n_month)]
    block_at = prov_at ^ (month * n_bin)
    sums = jax.ShapeDtypeStruct((n_bin, half, 2 * rank), jnp.float32)
    own_half, other_half = pl.pallas_call(
        first_product_kernel,
        out_shape=(sums, sums),
        in_specs=[smem, smem, hbm, vmem, vmem, vmem],
        out_specs=(vmem, vmem),
        scratch_shapes=tile_scratch,
        compiler_params=LARGE,
        name="first_product",
    )(block_at, month_at, tile_values, kept, slab_c, slab_b)

    pair_a = own_half + lax.ppermute(other_half, "month", swap)
    twice_b, pairs_c, pair_a = lax.optimization_barrier((twice_b, pairs_c, pair_a))
    own_a = lax.all_to_all(pair_a, BIN, 0, 0, tiled=True)

    square = jax.ShapeDtypeStruct((rank, rank), jnp.float32)
    inverse, gram_b = pl.pallas_call(
        first_inverse_kernel,
        out_shape=(square, square),
        cost_estimate=pl.CostEstimate(flops=20000000, bytes_accessed=200000, transcendentals=0),
        name="first_inverse",
        compiler_params=SMALL,
    )(twice_b, pairs_c)
    spread, factor_a = pl.pallas_call(
        solve_kernel,
        out_shape=(
            jax.ShapeDtypeStruct(own_a.shape, jnp.float32),
            jax.ShapeDtypeStruct((tile_i, rank), jnp.float32),
        ),
        compiler_params=SMALL,
        name="solve_first",
    )(own_a, inverse)

    half_a = lax.all_to_all(spread, BIN, 0, 0, tiled=True)
    other_a = lax.ppermute(half_a, "month", swap)

    n_out = n_prov * n_month
    out_rows = tile_k // n_out
    partial_c, packed = pl.pallas_call(
        last_product_kernel,
        out_shape=(
            jax.ShapeDtypeStruct((n_out, out_rows * rank), jnp.float32),
            jax.ShapeDtypeStruct((rank // 8 + 1, 2 * rank), jnp.float32),
        ),
        in_specs=[smem, smem, hbm, vmem, vmem, vmem, vmem],
        out_specs=(vmem, vmem),
        scratch_shapes=tile_scratch + [pltpu.VMEM((tile_k, rank), jnp.float32)],
        compiler_params=LARGE,
        name="last_product",
    )(block_at, month_at, tile_values, kept, half_a, other_a, slab_b)

    sent_gram = jnp.broadcast_to(packed.reshape(1, 1, -1), (n_out, 1, packed.size))
    last = jnp.concatenate([partial_c[:, None, :], sent_gram], axis=2)
    last = lax.all_to_all(last, PROV + ("month",), 0, 0, tiled=True)
    new_c = pl.pallas_call(
        last_kernel,
        out_shape=jax.ShapeDtypeStruct((out_rows, rank), jnp.float32),
        compiler_params=SMALL,
        name="last_solve",
    )(last.reshape(n_out, -1), gram_b)
    return (factor_a, new_c)


def solution(mesh):
    prov, month, bins = mesh.devices.shape
    shape = (prov // 8, 8, month, bins // 2, 2)
    mesh = jax.sharding.Mesh(mesh.devices.reshape(shape), ("zl", "y", "month", "x", "zh"))
    everywhere = PROV + ("month",) + BIN
    in_specs = (
        P(everywhere, None, None, None),
        P(everywhere),
        P(everywhere),
        P(PROV + ("month",), None),
        P(PROV + BIN, None),
    )
    out_specs = (P(everywhere, None), P(BIN + PROV + ("month",), None))
    return jax.shard_map(shards, mesh=mesh, in_specs=in_specs, out_specs=out_specs, check_vma=False)
```

```python
import jax
import jax.numpy as jnp
from jax import lax
from jax.experimental import pallas as pl
from jax.experimental.pallas import tpu as pltpu
from jax.sharding import PartitionSpec as P

MB_DEV = 8
KEPT = 5
PB_DEV = 16
epsilon = 1e-06
HIGH = lax.Precision.HIGHEST
SMALL = pltpu.CompilerParams(vmem_limit_bytes=8 * 1024 * 1024)
LARGE = pltpu.CompilerParams(vmem_limit_bytes=50 * 1024 * 1024)
PROV = ("zl", "y")
BIN = ("x", "zh")


def dot32(a, b, dims, precision=HIGH):
    return lax.dot_general(a, b, (dims, ((), ())), precision=precision, preferred_element_type=jnp.float32)


def diagonals(a):
    lane = lax.broadcasted_iota(jnp.int32, a.shape, 1)
    sub = lax.broadcasted_iota(jnp.int32, a.shape, 0)
    diag = jnp.where(lane == sub, a, 0.0)
    return jnp.sum(diag, axis=0, keepdims=True), jnp.sum(diag, axis=1, keepdims=True)


def spd_inverse(a):
    n = a.shape[0]
    in_row, in_col = diagonals(a)
    in_row, in_col = lax.rsqrt(in_row), lax.rsqrt(in_col)
    a = a * in_col * in_row
    lane = lax.broadcasted_iota(jnp.int32, a.shape, 1)
    sub = lax.broadcasted_iota(jnp.int32, a.shape, 0)
    lane_row = lax.broadcasted_iota(jnp.int32, (1, n), 1)
    for k in range(0, n, 4):
        cols = [jnp.broadcast_to(a[:, k + j : k + j + 1], a.shape) for j in range(4)]
        (p00, p01, p02, p03), (_, p11, p12, p13), (_, _, p22, p23), (_, _, _, p33) = [
            [cols[j][k + i : k + i + 1] for j in range(4)] for i in range(4)
        ]
        inv = 1.0 / (p00 * p11 - p01 * p01)
        e00, e01, e11 = p11 * inv, -p01 * inv, p00 * inv
        w00, w01 = e00 * p02 + e01 * p12, e00 * p03 + e01 * p13
        w10, w11 = e01 * p02 + e11 * p12, e01 * p03 + e11 * p13
        s00, s01 = p22 - (p02 * w00 + p12 * w10), p23 - (p02 * w01 + p12 * w11)
        s11 = p33 - (p03 * w01 + p13 * w11)
        inv = 1.0 / (s00 * s11 - s01 * s01)
        q22, q23, q33 = s11 * inv, -s01 * inv, s00 * inv
        v00, v01 = w00 * q22 + w01 * q23, w00 * q23 + w01 * q33
        v10, v11 = w10 * q22 + w11 * q23, w10 * q23 + w11 * q33
        q01 = e01 + v00 * w10 + v01 * w11
        pivot = (
            (e00 + v00 * w00 + v01 * w01, q01, -v00, -v01),
            (q01, e11 + v10 * w10 + v11 * w11, -v10, -v11),
            (-v00, -v10, q22, q23),
            (-v01, -v11, q23, q33),
        )
        rows = [a[k + j : k + j + 1] for j in range(4)]
        rest = jnp.where((lane >= k) & (lane < k + 4), 0.0, a)
        fresh = []
        for i in range(4):
            q = pivot[i]
            new = (q[0] * rows[0] + q[1] * rows[1]) + (q[2] * rows[2] + q[3] * rows[3])
            for j in range(4):
                new = jnp.where(lane_row == k + j, q[j], new)
            fresh.append(new)
        a = rest - ((cols[0] * fresh[0] + cols[1] * fresh[1]) + (cols[2] * fresh[2] + cols[3] * fresh[3]))
        for i in range(4):
            a = jnp.where(sub == k + i, fresh[i], a)
    return a * in_col * in_row


def first_inverse_kernel(b_ref, pairs_ref, inv_ref, gram_b_ref):
    rank = inv_ref.shape[0]
    b = b_ref[:, :rank]
    gram_b = dot32(b, b, ((0,), (0,)), None)
    z = pairs_ref[...]
    twin = dot32(z, z, ((0,), (0,)), None)
    gram_c = twin[:rank, :rank] + twin[rank:, rank:]
    gram_b_ref[...] = gram_b
    inv_ref[...] = spd_inverse(gram_b * gram_c)


def spread_kernel(c_ref, b_ref, out_ref, chunk, sems):
    month = lax.axis_index("month")
    bin_at = lax.axis_index("x") * lax.axis_size("zh") + lax.axis_index("zh")
    c, b = c_ref[...].astype(jnp.float32), b_ref[...].astype(jnp.float32)
    rows = lax.broadcasted_iota(jnp.int32, c.shape, 0)

    def row(values, at):
        return jnp.sum(jnp.where(rows == at, values, 0.0), axis=0, keepdims=True)

    c_rows = c.shape[0] // lax.axis_size("month")
    b_row = row(b, bin_at // (lax.axis_size(BIN) // b.shape[0]))
    first = jnp.concatenate([row(c, month * c_rows + k) for k in range(c_rows)], axis=1)
    both = jnp.concatenate([first] + [jnp.concatenate([b_row] * c_rows, axis=1)], axis=0)
    chunk[...] = jnp.broadcast_to(both.astype(chunk.dtype)[None], chunk.shape)
    size = chunk.shape[0]
    copies = [
        pltpu.make_async_copy(chunk, out_ref.at[pl.ds(k * size, size)], sems.at[k]) for k in range(out_ref.shape[0] // size)
    ]
    for copy in copies:
        copy.start()
    for copy in copies:
        copy.wait()


def keep_kernel(tiles_ref, kept_ref, sem):
    copy = pltpu.make_async_copy(tiles_ref.at[pl.ds(0, kept_ref.shape[0])], kept_ref, sem)
    copy.start()
    copy.wait()


def tile_copies(tiles_ref, late, sems):
    kept = tiles_ref.shape[0] - late.shape[0]
    copies = [pltpu.make_async_copy(tiles_ref.at[kept + t], late.at[t], sems.at[t]) for t in range(late.shape[0])]
    for copy in copies:
        copy.start()
    return [None] * kept + copies


def both_halves(kept_ref, late, t, start, size):
    kept, tile_i, tile_j, tile_k = kept_ref.shape
    tile, at = (kept_ref, t) if t < kept else (late, t - kept)
    upper = tile[at, start : start + size].reshape(size * tile_j, tile_k)
    lower = tile[at, tile_i // 2 + start : tile_i // 2 + start + size].reshape(size * tile_j, tile_k)
    return jnp.concatenate([upper, lower], axis=1)


def first_product_kernel(at_ref, month_ref, tiles_ref, kept_ref, c_ref, b_ref, own_ref, other_ref, late, sems):
    copies = tile_copies(tiles_ref, late, sems)
    own_ref[...] = jnp.zeros_like(own_ref)
    other_ref[...] = jnp.zeros_like(other_ref)
    c = c_ref[...]
    blocks = own_ref.shape[0]
    zero = jnp.zeros_like(c)
    twice_c = jnp.concatenate([jnp.concatenate([c, zero], axis=1), jnp.concatenate([zero, c], axis=1)], axis=0)
    half, tile_j = tiles_ref.shape[1] // 2, tiles_ref.shape[2]
    size = half // 4
    for t, copy in enumerate(copies):
        if copy is not None:
            copy.wait()
        at = at_ref[t]
        b = b_ref[month_ref[t]][None]
        for start in range(0, half, size):
            product = dot32(both_halves(kept_ref, late, t, start, size), twice_c, ((1,), (0,)), None)
            product = product.reshape(size, tile_j, -1) * b
            product = jnp.sum(product, axis=1)
            rows = pl.ds(start, size)
            own_ref[at % blocks, rows] += jnp.where(at < blocks, product, 0.0)
            other_ref[at % blocks, rows] += jnp.where(at < blocks, 0.0, product)


def solve_kernel(got_ref, inv_ref, out_ref, own_ref):
    rank = inv_ref.shape[0]
    total = got_ref[0]
    for source in range(1, got_ref.shape[0]):
        total = total + got_ref[source]
    inv = inv_ref[...]
    upper = dot32(total[:, :rank], inv, ((1,), (0,)))
    lower = dot32(total[:, rank:], inv, ((1,), (0,)))
    solved = jnp.concatenate([upper, lower], axis=1)
    for target in range(out_ref.shape[0]):
        out_ref[target] = solved
    own_ref[: upper.shape[0]] = upper
    own_ref[upper.shape[0] :] = lower


def iotas(n):
    return lax.broadcasted_iota(jnp.int32, (n, n), 0), lax.broadcasted_iota(jnp.int32, (n, n), 1)


def pack_gram(gram, month):
    n = gram.shape[0] // 2
    row, column = iotas(n)
    last = gram[n:, n:]
    triangles = jnp.where(row >= column, gram[:n, :n], last)
    mine = jnp.where(month == 0, gram[:n, n:], triangles)
    per = n // 4
    folded = jnp.concatenate([mine[k * per : (k + 1) * per] for k in range(4)], axis=1)
    diagonal = jnp.sum(jnp.where(row == column, last, 0.0), axis=0, keepdims=True)
    return folded, jnp.concatenate([diagonal, jnp.zeros((1, 3 * n), jnp.float32)], axis=1)


def unpack_gram(block, triangles, diagonal):
    n = diagonal.shape[1]
    row, column = iotas(n)

    def square(flat):
        rows = jnp.concatenate([flat[:, k * 4 * n : (k + 1) * 4 * n] for k in range(n // 4)], axis=0)
        return jnp.concatenate([rows[:, k * n : (k + 1) * n] for k in range(4)], axis=0)

    block, triangles = square(block), square(triangles)
    turned = triangles.T
    first = jnp.where(row >= column, triangles, turned)
    last = jnp.where(row < column, triangles, jnp.where(row > column, turned, diagonal))
    return jnp.concatenate(
        [jnp.concatenate([first, block], axis=1), jnp.concatenate([block.T, last], axis=1)], axis=0
    )


def last_product_kernel(at_ref, month_ref, tiles_ref, kept_ref, a_ref, other_ref, b_ref, out_ref, gram_ref, late, sems, turned):
    copies = tile_copies(tiles_ref, late, sems)
    blocks, half, lanes = a_ref.shape
    rank, tile_j, tile_k = lanes // 2, tiles_ref.shape[2], tiles_ref.shape[3]
    size = half // 4
    own, other = (ref[...].reshape(blocks * half, lanes) for ref in (a_ref, other_ref))
    twin = dot32(own, own, ((0,), (0,))) + dot32(other, other, ((0,), (0,)))
    folded, diagonal = pack_gram(twin[:rank, :rank] + twin[rank:, rank:], month_ref[month_ref.shape[0] - 1])
    gram_ref[: folded.shape[0]] = folded
    gram_ref[folded.shape[0] :] = diagonal
    total = None
    for t, copy in enumerate(copies):
        if copy is not None:
            copy.wait()
        at = at_ref[t]
        b = b_ref[month_ref[t]][None]
        for start in range(0, half, size):
            rows = pl.ds(start, size)
            a = jnp.where(at < blocks, a_ref[at % blocks, rows], other_ref[at % blocks, rows])
            joint = (a[:, None, :] * b).reshape(size * tile_j, lanes).T
            high = joint.astype(jnp.bfloat16)
            low = (joint - high.astype(jnp.float32)).astype(jnp.bfloat16)
            both = jnp.concatenate([high, low], axis=0)
            part = dot32(both, both_halves(kept_ref, late, t, start, size), ((1,), (0,)), None)
            total = part if total is None else total + part
    parts = [total[k * rank : (k + 1) * rank, (k % 2) * tile_k : (k % 2 + 1) * tile_k] for k in range(4)]
    turned[...] = (parts[0] + parts[1] + parts[2] + parts[3]).T
    out_rows = lanes // rank
    for row in range(out_rows):
        out_ref[:, row * rank : (row + 1) * rank] = turned[pl.ds(row, tile_k // out_rows, stride=out_rows), :]


def last_kernel(got_ref, gram_b_ref, out_ref):
    rank = gram_b_ref.shape[0]
    width = got_ref.shape[1]
    lead = out_ref.shape[0] * rank
    got = got_ref[...]
    total = jnp.sum(got.reshape(got.shape[0] // 8, 8, width), axis=0)
    total = (total[0:2] + total[2:4]) + (total[4:6] + total[6:8])
    rows = total[0:1, :lead] + total[1:2, :lead]
    own = jnp.concatenate([rows[:, j * rank : (j + 1) * rank] for j in range(out_ref.shape[0])], axis=0)
    end = lead + rank * rank // 4
    gram = unpack_gram(total[0:1, lead:end], total[1:2, lead:end], total[1:2, end : end + rank // 2])
    square_row, square_col = diagonals(gram)
    scale_row = jnp.sqrt(square_row + epsilon)
    scale_col = jnp.sqrt(square_col + epsilon)
    system = gram / scale_col / scale_row * gram_b_ref[...]
    out_ref[...] = dot32(own / scale_row, spd_inverse(system), ((1,), (0,)))


def shards(tile_values, prov_block, month_block, factor_b, factor_c):
    tiles, tile_i, tile_j, tile_k = tile_values.shape
    rank = factor_b.shape[1]
    n_prov = lax.axis_size(PROV)
    n_month = lax.axis_size("month")
    n_bin = lax.axis_size(BIN)
    month = lax.axis_index("month")
    bin_at = lax.axis_index(BIN)

    n_all = n_prov * n_month * n_bin
    c_rows = factor_c.shape[0] // n_month
    b_rep = n_bin // factor_b.shape[0]
    parts = 8
    sent = pl.pallas_call(
        spread_kernel,
        out_shape=jax.ShapeDtypeStruct((n_all, 2, c_rows * rank), factor_c.dtype),
        in_specs=[pl.BlockSpec(memory_space=pltpu.VMEM)] * 2,
        out_specs=pl.BlockSpec(memory_space=pl.ANY),
        scratch_shapes=[
            pltpu.VMEM((n_all // parts, 2, c_rows * rank), factor_c.dtype),
            pltpu.SemaphoreType.DMA((parts,)),
        ],
        compiler_params=pltpu.CompilerParams(vmem_limit_bytes=60 * 1024 * 1024),
        name="spread_rows",
    )(factor_c, factor_b)
    got = lax.all_to_all(sent, PROV + BIN + ("month",), 0, 0, tiled=True)
    pairs_c = got[:, 0, :]
    twice_b = got[:, 1, :].reshape(n_prov, factor_b.shape[0], b_rep, n_month, c_rows * rank)[:, :, 0]
    twice_b = twice_b.transpose(0, 2, 1, 3).reshape(-1, c_rows * rank)

    slab_pairs = lax.dynamic_slice_in_dim(pairs_c, bin_at * (tile_k // c_rows), tile_k // c_rows, 0)
    slab_c = slab_pairs.reshape(tile_k, rank)
    slab_b = lax.dynamic_slice_in_dim(twice_b, month * (MB_DEV * tile_j), MB_DEV * tile_j, 0)
    slab_b = slab_b.astype(jnp.float32).reshape(MB_DEV, tile_j, c_rows * rank)

    smem, vmem, hbm = (pl.BlockSpec(memory_space=space) for space in (pltpu.SMEM, pltpu.VMEM, pl.ANY))
    kept = pl.pallas_call(
        keep_kernel,
        out_shape=jax.ShapeDtypeStruct((KEPT,) + tile_values.shape[1:], tile_values.dtype),
        in_specs=[hbm],
        out_specs=vmem,
        scratch_shapes=[pltpu.SemaphoreType.DMA],
        compiler_params=LARGE,
        name="keep_tiles",
    )(tile_values)
    late = tiles - KEPT
    tile_scratch = [
        pltpu.VMEM((late,) + tile_values.shape[1:], tile_values.dtype),
        pltpu.SemaphoreType.DMA((late,)),
    ]
    half = tile_i // 2
    prov_at = jnp.clip(prov_block, 0, PB_DEV - 1)
    month_at = jnp.clip(jnp.concatenate([month_block, month[None]]), 0, MB_DEV - 1)
    swap = [(i, n_month - 1 - i) for i in range(n_month)]
    block_at = prov_at ^ (month * n_bin)
    sums = jax.ShapeDtypeStruct((n_bin, half, 2 * rank), jnp.float32)
    own_half, other_half = pl.pallas_call(
        first_product_kernel,
        out_shape=(sums, sums),
        in_specs=[smem, smem, hbm, vmem, vmem, vmem],
        out_specs=(vmem, vmem),
        scratch_shapes=tile_scratch,
        compiler_params=LARGE,
        name="first_product",
    )(block_at, month_at, tile_values, kept, slab_c, slab_b)

    pair_a = own_half + lax.ppermute(other_half, "month", swap)
    twice_b, pairs_c, pair_a = lax.optimization_barrier((twice_b, pairs_c, pair_a))
    own_a = lax.all_to_all(pair_a, BIN, 0, 0, tiled=True)

    square = jax.ShapeDtypeStruct((rank, rank), jnp.float32)
    inverse, gram_b = pl.pallas_call(
        first_inverse_kernel,
        out_shape=(square, square),
        cost_estimate=pl.CostEstimate(flops=20000000, bytes_accessed=200000, transcendentals=0),
        name="first_inverse",
        compiler_params=SMALL,
    )(twice_b, pairs_c)
    spread, factor_a = pl.pallas_call(
        solve_kernel,
        out_shape=(
            jax.ShapeDtypeStruct(own_a.shape, jnp.float32),
            jax.ShapeDtypeStruct((tile_i, rank), jnp.float32),
        ),
        compiler_params=SMALL,
        name="solve_first",
    )(own_a, inverse)

    half_a = lax.all_to_all(spread, BIN, 0, 0, tiled=True)
    other_a = lax.ppermute(half_a, "month", swap)

    n_out = n_prov * n_month
    out_rows = tile_k // n_out
    partial_c, packed = pl.pallas_call(
        last_product_kernel,
        out_shape=(
            jax.ShapeDtypeStruct((n_out, out_rows * rank), jnp.float32),
            jax.ShapeDtypeStruct((rank // 8 + 1, 2 * rank), jnp.float32),
        ),
        in_specs=[smem, smem, hbm, vmem, vmem, vmem, vmem],
        out_specs=(vmem, vmem),
        scratch_shapes=tile_scratch + [pltpu.VMEM((tile_k, rank), jnp.float32)],
        compiler_params=LARGE,
        name="last_product",
    )(block_at, month_at, tile_values, kept, half_a, other_a, slab_b)

    sent_gram = jnp.broadcast_to(packed.reshape(1, 1, -1), (n_out, 1, packed.size))
    last = jnp.concatenate([partial_c[:, None, :], sent_gram], axis=2)
    last = lax.all_to_all(last, PROV + ("month",), 0, 0, tiled=True)
    new_c = pl.pallas_call(
        last_kernel,
        out_shape=jax.ShapeDtypeStruct((out_rows, rank), jnp.float32),
        compiler_params=SMALL,
        name="last_solve",
    )(last.reshape(n_out, -1), gram_b)
    return (factor_a, new_c)


def solution(mesh):
    prov, month, bins = mesh.devices.shape
    shape = (prov // 8, 8, month, bins // 2, 2)
    mesh = jax.sharding.Mesh(mesh.devices.reshape(shape), ("zl", "y", "month", "x", "zh"))
    everywhere = PROV + ("month",) + BIN
    in_specs = (
        P(everywhere, None, None, None),
        P(everywhere),
        P(everywhere),
        P(PROV + ("month",), None),
        P(PROV + BIN, None),
    )
    out_specs = (P(everywhere, None), P(BIN + PROV + ("month",), None))
    return jax.shard_map(shards, mesh=mesh, in_specs=in_specs, out_specs=out_specs, check_vma=False)
```

```python
import jax
import jax.numpy as jnp
from jax import lax
from jax.experimental import pallas as pl
from jax.experimental.pallas import tpu as pltpu
from jax.sharding import PartitionSpec as P

MB_DEV = 8
KEPT = 5
PB_DEV = 16
epsilon = 1e-06
HIGH = lax.Precision.HIGHEST
SMALL = pltpu.CompilerParams(vmem_limit_bytes=8 * 1024 * 1024)
LARGE = pltpu.CompilerParams(vmem_limit_bytes=50 * 1024 * 1024)
PROV = ("zl", "y")
BIN = ("x", "zh")


def dot32(a, b, dims, precision=HIGH):
    return lax.dot_general(a, b, (dims, ((), ())), precision=precision, preferred_element_type=jnp.float32)


def diagonals(a):
    lane = lax.broadcasted_iota(jnp.int32, a.shape, 1)
    sub = lax.broadcasted_iota(jnp.int32, a.shape, 0)
    diag = jnp.where(lane == sub, a, 0.0)
    return jnp.sum(diag, axis=0, keepdims=True), jnp.sum(diag, axis=1, keepdims=True)


def spd_inverse(a):
    n = a.shape[0]
    in_row, in_col = diagonals(a)
    in_row, in_col = lax.rsqrt(in_row), lax.rsqrt(in_col)
    a = a * in_col * in_row
    lane = lax.broadcasted_iota(jnp.int32, a.shape, 1)
    sub = lax.broadcasted_iota(jnp.int32, a.shape, 0)
    lane_row = lax.broadcasted_iota(jnp.int32, (1, n), 1)
    for k in range(0, n, 4):
        cols = [jnp.broadcast_to(a[:, k + j : k + j + 1], a.shape) for j in range(4)]
        (p00, p01, p02, p03), (_, p11, p12, p13), (_, _, p22, p23), (_, _, _, p33) = [
            [cols[j][k + i : k + i + 1] for j in range(4)] for i in range(4)
        ]
        inv = 1.0 / (p00 * p11 - p01 * p01)
        e00, e01, e11 = p11 * inv, -p01 * inv, p00 * inv
        w00, w01 = e00 * p02 + e01 * p12, e00 * p03 + e01 * p13
        w10, w11 = e01 * p02 + e11 * p12, e01 * p03 + e11 * p13
        s00, s01 = p22 - (p02 * w00 + p12 * w10), p23 - (p02 * w01 + p12 * w11)
        s11 = p33 - (p03 * w01 + p13 * w11)
        inv = 1.0 / (s00 * s11 - s01 * s01)
        q22, q23, q33 = s11 * inv, -s01 * inv, s00 * inv
        v00, v01 = w00 * q22 + w01 * q23, w00 * q23 + w01 * q33
        v10, v11 = w10 * q22 + w11 * q23, w10 * q23 + w11 * q33
        q01 = e01 + v00 * w10 + v01 * w11
        pivot = (
            (e00 + v00 * w00 + v01 * w01, q01, -v00, -v01),
            (q01, e11 + v10 * w10 + v11 * w11, -v10, -v11),
            (-v00, -v10, q22, q23),
            (-v01, -v11, q23, q33),
        )
        rows = [a[k + j : k + j + 1] for j in range(4)]
        rest = jnp.where((lane >= k) & (lane < k + 4), 0.0, a)
        fresh = []
        for i in range(4):
            q = pivot[i]
            new = (q[0] * rows[0] + q[1] * rows[1]) + (q[2] * rows[2] + q[3] * rows[3])
            for j in range(4):
                new = jnp.where(lane_row == k + j, q[j], new)
            fresh.append(new)
        a = rest - ((cols[0] * fresh[0] + cols[1] * fresh[1]) + (cols[2] * fresh[2] + cols[3] * fresh[3]))
        for i in range(4):
            a = jnp.where(sub == k + i, fresh[i], a)
    return a * in_col * in_row


def first_inverse_kernel(b_ref, pairs_ref, inv_ref, gram_b_ref):
    rank = inv_ref.shape[0]
    b = b_ref[:, :rank]
    gram_b = dot32(b, b, ((0,), (0,)), None)
    z = pairs_ref[...]
    twin = dot32(z, z, ((0,), (0,)), None)
    gram_c = twin[:rank, :rank] + twin[rank:, rank:]
    gram_b_ref[...] = gram_b
    inv_ref[...] = spd_inverse(gram_b * gram_c)


def spread_kernel(c_ref, b_ref, out_ref, chunk, sems):
    month = lax.axis_index("month")
    bin_at = lax.axis_index("x") * lax.axis_size("zh") + lax.axis_index("zh")
    c, b = c_ref[...].astype(jnp.float32), b_ref[...].astype(jnp.float32)
    rows = lax.broadcasted_iota(jnp.int32, c.shape, 0)

    def row(values, at):
        return jnp.sum(jnp.where(rows == at, values, 0.0), axis=0, keepdims=True)

    c_rows = c.shape[0] // lax.axis_size("month")
    b_row = row(b, bin_at // (lax.axis_size(BIN) // b.shape[0]))
    first = jnp.concatenate([row(c, month * c_rows + k) for k in range(c_rows)], axis=1)
    both = jnp.concatenate([first] + [jnp.concatenate([b_row] * c_rows, axis=1)], axis=0)
    chunk[...] = jnp.broadcast_to(both.astype(chunk.dtype)[None], chunk.shape)
    size = chunk.shape[0]
    copies = [
        pltpu.make_async_copy(chunk, out_ref.at[pl.ds(k * size, size)], sems.at[k]) for k in range(out_ref.shape[0] // size)
    ]
    for copy in copies:
        copy.start()
    for copy in copies:
        copy.wait()


def keep_kernel(tiles_ref, kept_ref, sem):
    copy = pltpu.make_async_copy(tiles_ref.at[pl.ds(0, kept_ref.shape[0])], kept_ref, sem)
    copy.start()
    copy.wait()


def tile_copies(tiles_ref, late, sems):
    kept = tiles_ref.shape[0] - late.shape[0]
    copies = [pltpu.make_async_copy(tiles_ref.at[kept + t], late.at[t], sems.at[t]) for t in range(late.shape[0])]
    for copy in copies:
        copy.start()
    return [None] * kept + copies


def both_halves(kept_ref, late, t, start, size):
    kept, tile_i, tile_j, tile_k = kept_ref.shape
    tile, at = (kept_ref, t) if t < kept else (late, t - kept)
    upper = tile[at, start : start + size].reshape(size * tile_j, tile_k)
    lower = tile[at, tile_i // 2 + start : tile_i // 2 + start + size].reshape(size * tile_j, tile_k)
    return jnp.concatenate([upper, lower], axis=1)


def first_product_kernel(at_ref, month_ref, tiles_ref, kept_ref, c_ref, b_ref, own_ref, other_ref, late, sems):
    copies = tile_copies(tiles_ref, late, sems)
    own_ref[...] = jnp.zeros_like(own_ref)
    other_ref[...] = jnp.zeros_like(other_ref)
    c = c_ref[...]
    blocks = own_ref.shape[0]
    zero = jnp.zeros_like(c)
    twice_c = jnp.concatenate([jnp.concatenate([c, zero], axis=1), jnp.concatenate([zero, c], axis=1)], axis=0)
    half, tile_j = tiles_ref.shape[1] // 2, tiles_ref.shape[2]
    size = half // 4
    for t, copy in enumerate(copies):
        if copy is not None:
            copy.wait()
        at = at_ref[t]
        b = b_ref[month_ref[t]][None]
        for start in range(0, half, size):
            product = dot32(both_halves(kept_ref, late, t, start, size), twice_c, ((1,), (0,)), None)
            product = product.reshape(size, tile_j, -1) * b
            product = jnp.sum(product, axis=1)
            rows = pl.ds(start, size)
            own_ref[at % blocks, rows] += jnp.where(at < blocks, product, 0.0)
            other_ref[at % blocks, rows] += jnp.where(at < blocks, 0.0, product)


def solve_kernel(got_ref, inv_ref, out_ref, own_ref):
    rank = inv_ref.shape[0]
    total = got_ref[0]
    for source in range(1, got_ref.shape[0]):
        total = total + got_ref[source]
    inv = inv_ref[...]
    upper = dot32(total[:, :rank], inv, ((1,), (0,)))
    lower = dot32(total[:, rank:], inv, ((1,), (0,)))
    solved = jnp.concatenate([upper, lower], axis=1)
    for target in range(out_ref.shape[0]):
        out_ref[target] = solved
    own_ref[: upper.shape[0]] = upper
    own_ref[upper.shape[0] :] = lower


def iotas(n):
    return lax.broadcasted_iota(jnp.int32, (n, n), 0), lax.broadcasted_iota(jnp.int32, (n, n), 1)


def pack_gram(gram, month):
    n = gram.shape[0] // 2
    row, column = iotas(n)
    last = gram[n:, n:]
    triangles = jnp.where(row >= column, gram[:n, :n], last)
    mine = jnp.where(month == 0, gram[:n, n:], triangles)
    per = n // 4
    folded = jnp.concatenate([mine[k * per : (k + 1) * per] for k in range(4)], axis=1)
    diagonal = jnp.sum(jnp.where(row == column, last, 0.0), axis=0, keepdims=True)
    return folded, jnp.concatenate([diagonal, jnp.zeros((1, 3 * n), jnp.float32)], axis=1)


def unpack_gram(block, triangles, diagonal):
    n = diagonal.shape[1]
    row, column = iotas(n)

    def square(flat):
        rows = jnp.concatenate([flat[:, k * 4 * n : (k + 1) * 4 * n] for k in range(n // 4)], axis=0)
        return jnp.concatenate([rows[:, k * n : (k + 1) * n] for k in range(4)], axis=0)

    block, triangles = square(block), square(triangles)
    turned = triangles.T
    first = jnp.where(row >= column, triangles, turned)
    last = jnp.where(row < column, triangles, jnp.where(row > column, turned, diagonal))
    return jnp.concatenate(
        [jnp.concatenate([first, block], axis=1), jnp.concatenate([block.T, last], axis=1)], axis=0
    )


def last_product_kernel(at_ref, month_ref, tiles_ref, kept_ref, a_ref, other_ref, b_ref, out_ref, gram_ref, late, sems, turned):
    copies = tile_copies(tiles_ref, late, sems)
    blocks, half, lanes = a_ref.shape
    rank, tile_j, tile_k = lanes // 2, tiles_ref.shape[2], tiles_ref.shape[3]
    size = half // 4
    own, other = (ref[...].reshape(blocks * half, lanes) for ref in (a_ref, other_ref))
    twin = dot32(own, own, ((0,), (0,))) + dot32(other, other, ((0,), (0,)))
    folded, diagonal = pack_gram(twin[:rank, :rank] + twin[rank:, rank:], month_ref[month_ref.shape[0] - 1])
    gram_ref[: folded.shape[0]] = folded
    gram_ref[folded.shape[0] :] = diagonal
    total = None
    for t, copy in enumerate(copies):
        if copy is not None:
            copy.wait()
        at = at_ref[t]
        b = b_ref[month_ref[t]][None]
        for start in range(0, half, size):
            rows = pl.ds(start, size)
            a = jnp.where(at < blocks, a_ref[at % blocks, rows], other_ref[at % blocks, rows])
            joint = (a[:, None, :] * b).reshape(size * tile_j, lanes).T
            high = joint.astype(jnp.bfloat16)
            low = (joint - high.astype(jnp.float32)).astype(jnp.bfloat16)
            both = jnp.concatenate([high, low], axis=0)
            part = dot32(both, both_halves(kept_ref, late, t, start, size), ((1,), (0,)), None)
            total = part if total is None else total + part
    parts = [total[k * rank : (k + 1) * rank, (k % 2) * tile_k : (k % 2 + 1) * tile_k] for k in range(4)]
    turned[...] = (parts[0] + parts[1] + parts[2] + parts[3]).T
    out_rows = lanes // rank
    for row in range(out_rows):
        out_ref[:, row * rank : (row + 1) * rank] = turned[pl.ds(row, tile_k // out_rows, stride=out_rows), :]


def fold_kernel(got_ref, keep_ref, send_ref):
    lead = (got_ref.shape[1] - keep_ref.shape[1]) // (lax.axis_size("month") - 1)
    got = got_ref[...]
    total = jnp.sum(got.reshape(got.shape[0] // 8, 8, got.shape[1]), axis=0)
    total = jnp.sum(total, axis=0, keepdims=True)
    zero, one, half = total[:, :lead], total[:, lead : 2 * lead], total[:, 2 * lead :]
    first = lax.axis_index("month") == 0
    keep_ref[...] = jnp.concatenate([jnp.where(first, zero, one), half], axis=1)
    send_ref[...] = jnp.concatenate([jnp.where(first, one, zero), half], axis=1)


def last_kernel(keep_ref, swapped_ref, gram_b_ref, out_ref):
    rank = gram_b_ref.shape[0]
    lead = out_ref.shape[0] * rank
    keep, swapped = keep_ref[...], swapped_ref[...]
    rows = keep[:, :lead] + swapped[:, :lead]
    own = jnp.concatenate([rows[:, j * rank : (j + 1) * rank] for j in range(out_ref.shape[0])], axis=0)
    end = lead + rank * rank // 4
    first = lax.axis_index("month") == 0
    block, triangles = jnp.where(first, keep, swapped), jnp.where(first, swapped, keep)
    gram = unpack_gram(block[:, lead:end], triangles[:, lead:end], triangles[:, end : end + rank // 2])
    square_row, square_col = diagonals(gram)
    scale_row = jnp.sqrt(square_row + epsilon)
    scale_col = jnp.sqrt(square_col + epsilon)
    system = gram / scale_col / scale_row * gram_b_ref[...]
    out_ref[...] = dot32(own / scale_row, spd_inverse(system), ((1,), (0,)))


def shards(tile_values, prov_block, month_block, factor_b, factor_c):
    tiles, tile_i, tile_j, tile_k = tile_values.shape
    rank = factor_b.shape[1]
    n_prov = lax.axis_size(PROV)
    n_month = lax.axis_size("month")
    n_bin = lax.axis_size(BIN)
    month = lax.axis_index("month")
    bin_at = lax.axis_index(BIN)

    n_all = n_prov * n_month * n_bin
    c_rows = factor_c.shape[0] // n_month
    b_rep = n_bin // factor_b.shape[0]
    parts = 8
    sent = pl.pallas_call(
        spread_kernel,
        out_shape=jax.ShapeDtypeStruct((n_all, 2, c_rows * rank), factor_c.dtype),
        in_specs=[pl.BlockSpec(memory_space=pltpu.VMEM)] * 2,
        out_specs=pl.BlockSpec(memory_space=pl.ANY),
        scratch_shapes=[
            pltpu.VMEM((n_all // parts, 2, c_rows * rank), factor_c.dtype),
            pltpu.SemaphoreType.DMA((parts,)),
        ],
        compiler_params=pltpu.CompilerParams(vmem_limit_bytes=60 * 1024 * 1024),
        name="spread_rows",
    )(factor_c, factor_b)
    got = lax.all_to_all(sent, PROV + BIN + ("month",), 0, 0, tiled=True)
    pairs_c = got[:, 0, :]
    twice_b = got[:, 1, :].reshape(n_prov, factor_b.shape[0], b_rep, n_month, c_rows * rank)[:, :, 0]
    twice_b = twice_b.transpose(0, 2, 1, 3).reshape(-1, c_rows * rank)

    slab_pairs = lax.dynamic_slice_in_dim(pairs_c, bin_at * (tile_k // c_rows), tile_k // c_rows, 0)
    slab_c = slab_pairs.reshape(tile_k, rank)
    slab_b = lax.dynamic_slice_in_dim(twice_b, month * (MB_DEV * tile_j), MB_DEV * tile_j, 0)
    slab_b = slab_b.astype(jnp.float32).reshape(MB_DEV, tile_j, c_rows * rank)

    smem, vmem, hbm = (pl.BlockSpec(memory_space=space) for space in (pltpu.SMEM, pltpu.VMEM, pl.ANY))
    kept = pl.pallas_call(
        keep_kernel,
        out_shape=jax.ShapeDtypeStruct((KEPT,) + tile_values.shape[1:], tile_values.dtype),
        in_specs=[hbm],
        out_specs=vmem,
        scratch_shapes=[pltpu.SemaphoreType.DMA],
        compiler_params=LARGE,
        name="keep_tiles",
    )(tile_values)
    late = tiles - KEPT
    tile_scratch = [
        pltpu.VMEM((late,) + tile_values.shape[1:], tile_values.dtype),
        pltpu.SemaphoreType.DMA((late,)),
    ]
    half = tile_i // 2
    prov_at = jnp.clip(prov_block, 0, PB_DEV - 1)
    month_at = jnp.clip(jnp.concatenate([month_block, month[None]]), 0, MB_DEV - 1)
    swap = [(i, n_month - 1 - i) for i in range(n_month)]
    block_at = prov_at ^ (month * n_bin)
    sums = jax.ShapeDtypeStruct((n_bin, half, 2 * rank), jnp.float32)
    own_half, other_half = pl.pallas_call(
        first_product_kernel,
        out_shape=(sums, sums),
        in_specs=[smem, smem, hbm, vmem, vmem, vmem],
        out_specs=(vmem, vmem),
        scratch_shapes=tile_scratch,
        compiler_params=LARGE,
        name="first_product",
    )(block_at, month_at, tile_values, kept, slab_c, slab_b)

    pair_a = own_half + lax.ppermute(other_half, "month", swap)
    twice_b, pairs_c, pair_a = lax.optimization_barrier((twice_b, pairs_c, pair_a))
    own_a = lax.all_to_all(pair_a, BIN, 0, 0, tiled=True)

    square = jax.ShapeDtypeStruct((rank, rank), jnp.float32)
    inverse, gram_b = pl.pallas_call(
        first_inverse_kernel,
        out_shape=(square, square),
        cost_estimate=pl.CostEstimate(flops=20000000, bytes_accessed=200000, transcendentals=0),
        name="first_inverse",
        compiler_params=SMALL,
    )(twice_b, pairs_c)
    spread, factor_a = pl.pallas_call(
        solve_kernel,
        out_shape=(
            jax.ShapeDtypeStruct(own_a.shape, jnp.float32),
            jax.ShapeDtypeStruct((tile_i, rank), jnp.float32),
        ),
        compiler_params=SMALL,
        name="solve_first",
    )(own_a, inverse)

    half_a = lax.all_to_all(spread, BIN, 0, 0, tiled=True)
    other_a = lax.ppermute(half_a, "month", swap)

    n_out = n_prov * n_month
    out_rows = tile_k // n_out
    partial_c, packed = pl.pallas_call(
        last_product_kernel,
        out_shape=(
            jax.ShapeDtypeStruct((n_out, out_rows * rank), jnp.float32),
            jax.ShapeDtypeStruct((rank // 8 + 1, 2 * rank), jnp.float32),
        ),
        in_specs=[smem, smem, hbm, vmem, vmem, vmem, vmem],
        out_specs=(vmem, vmem),
        scratch_shapes=tile_scratch + [pltpu.VMEM((tile_k, rank), jnp.float32)],
        compiler_params=LARGE,
        name="last_product",
    )(block_at, month_at, tile_values, kept, half_a, other_a, slab_b)

    sent_gram = jnp.broadcast_to(packed.reshape(1, 1, -1), (n_prov, 1, packed.size))
    last = jnp.concatenate([partial_c.reshape(n_prov, 1, -1), sent_gram], axis=2)
    last = lax.all_to_all(last, PROV, 0, 0, tiled=True)
    summed = jax.ShapeDtypeStruct((1, out_rows * rank + packed.size), jnp.float32)
    keep, send = pl.pallas_call(
        fold_kernel, out_shape=(summed, summed), compiler_params=SMALL, name="fold_sources"
    )(last.reshape(n_prov, -1))
    new_c = pl.pallas_call(
        last_kernel,
        out_shape=jax.ShapeDtypeStruct((out_rows, rank), jnp.float32),
        compiler_params=SMALL,
        name="last_solve",
    )(keep, lax.ppermute(send, "month", swap), gram_b)
    return (factor_a, new_c)


def solution(mesh):
    prov, month, bins = mesh.devices.shape
    shape = (prov // 8, 8, month, bins // 2, 2)
    mesh = jax.sharding.Mesh(mesh.devices.reshape(shape), ("zl", "y", "month", "x", "zh"))
    everywhere = PROV + ("month",) + BIN
    in_specs = (
        P(everywhere, None, None, None),
        P(everywhere),
        P(everywhere),
        P(PROV + ("month",), None),
        P(PROV + BIN, None),
    )
    out_specs = (P(everywhere, None), P(BIN + PROV + ("month",), None))
    return jax.shard_map(shards, mesh=mesh, in_specs=in_specs, out_specs=out_specs, check_vma=False)
```

```python
import jax
import jax.numpy as jnp
from jax import lax
from jax.experimental import pallas as pl
from jax.experimental.pallas import tpu as pltpu
from jax.sharding import PartitionSpec as P

MB_DEV = 8
KEPT = 6
PB_DEV = 16
epsilon = 1e-06
HIGH = lax.Precision.HIGHEST
SMALL = pltpu.CompilerParams(vmem_limit_bytes=8 * 1024 * 1024)
LARGE = pltpu.CompilerParams(vmem_limit_bytes=50 * 1024 * 1024)
PROV = ("zl", "y")
BIN = ("x", "zh")


def dot32(a, b, dims, precision=HIGH):
    return lax.dot_general(a, b, (dims, ((), ())), precision=precision, preferred_element_type=jnp.float32)


def diagonals(a):
    lane = lax.broadcasted_iota(jnp.int32, a.shape, 1)
    sub = lax.broadcasted_iota(jnp.int32, a.shape, 0)
    diag = jnp.where(lane == sub, a, 0.0)
    return jnp.sum(diag, axis=0, keepdims=True), jnp.sum(diag, axis=1, keepdims=True)


def spd_inverse(a):
    n = a.shape[0]
    in_row, in_col = diagonals(a)
    in_row, in_col = lax.rsqrt(in_row), lax.rsqrt(in_col)
    a = a * in_col * in_row
    lane = lax.broadcasted_iota(jnp.int32, a.shape, 1)
    sub = lax.broadcasted_iota(jnp.int32, a.shape, 0)
    lane_row = lax.broadcasted_iota(jnp.int32, (1, n), 1)
    for k in range(0, n, 4):
        cols = [jnp.broadcast_to(a[:, k + j : k + j + 1], a.shape) for j in range(4)]
        (p00, p01, p02, p03), (_, p11, p12, p13), (_, _, p22, p23), (_, _, _, p33) = [
            [cols[j][k + i : k + i + 1] for j in range(4)] for i in range(4)
        ]
        inv = 1.0 / (p00 * p11 - p01 * p01)
        e00, e01, e11 = p11 * inv, -p01 * inv, p00 * inv
        w00, w01 = e00 * p02 + e01 * p12, e00 * p03 + e01 * p13
        w10, w11 = e01 * p02 + e11 * p12, e01 * p03 + e11 * p13
        s00, s01 = p22 - (p02 * w00 + p12 * w10), p23 - (p02 * w01 + p12 * w11)
        s11 = p33 - (p03 * w01 + p13 * w11)
        inv = 1.0 / (s00 * s11 - s01 * s01)
        q22, q23, q33 = s11 * inv, -s01 * inv, s00 * inv
        v00, v01 = w00 * q22 + w01 * q23, w00 * q23 + w01 * q33
        v10, v11 = w10 * q22 + w11 * q23, w10 * q23 + w11 * q33
        q01 = e01 + v00 * w10 + v01 * w11
        pivot = (
            (e00 + v00 * w00 + v01 * w01, q01, -v00, -v01),
            (q01, e11 + v10 * w10 + v11 * w11, -v10, -v11),
            (-v00, -v10, q22, q23),
            (-v01, -v11, q23, q33),
        )
        rows = [a[k + j : k + j + 1] for j in range(4)]
        rest = jnp.where((lane >= k) & (lane < k + 4), 0.0, a)
        fresh = []
        for i in range(4):
            q = pivot[i]
            new = (q[0] * rows[0] + q[1] * rows[1]) + (q[2] * rows[2] + q[3] * rows[3])
            for j in range(4):
                new = jnp.where(lane_row == k + j, q[j], new)
            fresh.append(new)
        a = rest - ((cols[0] * fresh[0] + cols[1] * fresh[1]) + (cols[2] * fresh[2] + cols[3] * fresh[3]))
        for i in range(4):
            a = jnp.where(sub == k + i, fresh[i], a)
    return a * in_col * in_row


def first_inverse_kernel(b_ref, pairs_ref, inv_ref, gram_b_ref):
    rank = inv_ref.shape[0]
    b = b_ref[:, :rank]
    gram_b = dot32(b, b, ((0,), (0,)), None)
    z = pairs_ref[...]
    twin = dot32(z, z, ((0,), (0,)), None)
    gram_c = twin[:rank, :rank] + twin[rank:, rank:]
    gram_b_ref[...] = gram_b
    inv_ref[...] = spd_inverse(gram_b * gram_c)


def spread_kernel(c_ref, b_ref, out_ref, chunk, sems):
    month = lax.axis_index("month")
    bin_at = lax.axis_index("x") * lax.axis_size("zh") + lax.axis_index("zh")
    c, b = c_ref[...].astype(jnp.float32), b_ref[...].astype(jnp.float32)
    rows = lax.broadcasted_iota(jnp.int32, c.shape, 0)

    def row(values, at):
        return jnp.sum(jnp.where(rows == at, values, 0.0), axis=0, keepdims=True)

    c_rows = c.shape[0] // lax.axis_size("month")
    b_row = row(b, bin_at // (lax.axis_size(BIN) // b.shape[0]))
    first = jnp.concatenate([row(c, month * c_rows + k) for k in range(c_rows)], axis=1)
    both = jnp.concatenate([first] + [jnp.concatenate([b_row] * c_rows, axis=1)], axis=0)
    chunk[...] = jnp.broadcast_to(both.astype(chunk.dtype)[None], chunk.shape)
    size = chunk.shape[0]
    copies = [
        pltpu.make_async_copy(chunk, out_ref.at[pl.ds(k * size, size)], sems.at[k]) for k in range(out_ref.shape[0] // size)
    ]
    for copy in copies:
        copy.start()
    for copy in copies:
        copy.wait()


def keep_kernel(tiles_ref, kept_ref, sem):
    copy = pltpu.make_async_copy(tiles_ref.at[pl.ds(0, kept_ref.shape[0])], kept_ref, sem)
    copy.start()
    copy.wait()


def tile_copies(tiles_ref, late, sems):
    kept = tiles_ref.shape[0] - late.shape[0]
    copies = [pltpu.make_async_copy(tiles_ref.at[kept + t], late.at[t], sems.at[t]) for t in range(late.shape[0])]
    for copy in copies:
        copy.start()
    return [None] * kept + copies


def both_halves(kept_ref, late, t, start, size):
    kept, tile_i, tile_j, tile_k = kept_ref.shape
    tile, at = (kept_ref, t) if t < kept else (late, t - kept)
    upper = tile[at, start : start + size].reshape(size * tile_j, tile_k)
    lower = tile[at, tile_i // 2 + start : tile_i // 2 + start + size].reshape(size * tile_j, tile_k)
    return jnp.concatenate([upper, lower], axis=1)


def first_product_kernel(at_ref, month_ref, tiles_ref, kept_ref, c_ref, b_ref, own_ref, other_ref, late, sems):
    copies = tile_copies(tiles_ref, late, sems)
    own_ref[...] = jnp.zeros_like(own_ref)
    other_ref[...] = jnp.zeros_like(other_ref)
    c = c_ref[...]
    blocks = own_ref.shape[0]
    zero = jnp.zeros_like(c)
    twice_c = jnp.concatenate([jnp.concatenate([c, zero], axis=1), jnp.concatenate([zero, c], axis=1)], axis=0)
    half, tile_j = tiles_ref.shape[1] // 2, tiles_ref.shape[2]
    size = half // 4
    for t, copy in enumerate(copies):
        if copy is not None:
            copy.wait()
        at = at_ref[t]
        b = b_ref[month_ref[t]][None]
        for start in range(0, half, size):
            product = dot32(both_halves(kept_ref, late, t, start, size), twice_c, ((1,), (0,)), None)
            product = product.reshape(size, tile_j, -1) * b
            product = jnp.sum(product, axis=1)
            rows = pl.ds(start, size)
            own_ref[at % blocks, rows] += jnp.where(at < blocks, product, 0.0)
            other_ref[at % blocks, rows] += jnp.where(at < blocks, 0.0, product)


def solve_kernel(got_ref, inv_ref, out_ref, own_ref):
    rank = inv_ref.shape[0]
    total = got_ref[0]
    for source in range(1, got_ref.shape[0]):
        total = total + got_ref[source]
    inv = inv_ref[...]
    upper = dot32(total[:, :rank], inv, ((1,), (0,)))
    lower = dot32(total[:, rank:], inv, ((1,), (0,)))
    solved = jnp.concatenate([upper, lower], axis=1)
    for target in range(out_ref.shape[0]):
        out_ref[target] = solved
    own_ref[: upper.shape[0]] = upper
    own_ref[upper.shape[0] :] = lower


def iotas(n):
    return lax.broadcasted_iota(jnp.int32, (n, n), 0), lax.broadcasted_iota(jnp.int32, (n, n), 1)


def pack_gram(gram, month):
    n = gram.shape[0] // 2
    row, column = iotas(n)
    last = gram[n:, n:]
    triangles = jnp.where(row >= column, gram[:n, :n], last)
    mine = jnp.where(month == 0, gram[:n, n:], triangles)
    per = n // 4
    folded = jnp.concatenate([mine[k * per : (k + 1) * per] for k in range(4)], axis=1)
    diagonal = jnp.sum(jnp.where(row == column, last, 0.0), axis=0, keepdims=True)
    return folded, jnp.concatenate([diagonal, jnp.zeros((1, 3 * n), jnp.float32)], axis=1)


def unpack_gram(block, triangles, diagonal):
    n = diagonal.shape[1]
    row, column = iotas(n)

    def square(flat):
        rows = jnp.concatenate([flat[:, k * 4 * n : (k + 1) * 4 * n] for k in range(n // 4)], axis=0)
        return jnp.concatenate([rows[:, k * n : (k + 1) * n] for k in range(4)], axis=0)

    block, triangles = square(block), square(triangles)
    turned = triangles.T
    first = jnp.where(row >= column, triangles, turned)
    last = jnp.where(row < column, triangles, jnp.where(row > column, turned, diagonal))
    return jnp.concatenate(
        [jnp.concatenate([first, block], axis=1), jnp.concatenate([block.T, last], axis=1)], axis=0
    )


def last_product_kernel(at_ref, month_ref, tiles_ref, kept_ref, a_ref, other_ref, b_ref, out_ref, gram_ref, late, sems, turned):
    copies = tile_copies(tiles_ref, late, sems)
    blocks, half, lanes = a_ref.shape
    rank, tile_j, tile_k = lanes // 2, tiles_ref.shape[2], tiles_ref.shape[3]
    size = half // 4
    own, other = (ref[...].reshape(blocks * half, lanes) for ref in (a_ref, other_ref))
    twin = dot32(own, own, ((0,), (0,))) + dot32(other, other, ((0,), (0,)))
    folded, diagonal = pack_gram(twin[:rank, :rank] + twin[rank:, rank:], month_ref[month_ref.shape[0] - 1])
    gram_ref[: folded.shape[0]] = folded
    gram_ref[folded.shape[0] :] = diagonal
    total = None
    for t, copy in enumerate(copies):
        if copy is not None:
            copy.wait()
        at = at_ref[t]
        b = b_ref[month_ref[t]][None]
        for start in range(0, half, size):
            rows = pl.ds(start, size)
            a = jnp.where(at < blocks, a_ref[at % blocks, rows], other_ref[at % blocks, rows])
            joint = (a[:, None, :] * b).reshape(size * tile_j, lanes).T
            high = joint.astype(jnp.bfloat16)
            low = (joint - high.astype(jnp.float32)).astype(jnp.bfloat16)
            both = jnp.concatenate([high, low], axis=0)
            part = dot32(both, both_halves(kept_ref, late, t, start, size), ((1,), (0,)), None)
            total = part if total is None else total + part
    parts = [total[k * rank : (k + 1) * rank, (k % 2) * tile_k : (k % 2 + 1) * tile_k] for k in range(4)]
    turned[...] = (parts[0] + parts[1] + parts[2] + parts[3]).T
    out_rows = lanes // rank
    for row in range(out_rows):
        out_ref[:, row * rank : (row + 1) * rank] = turned[pl.ds(row, tile_k // out_rows, stride=out_rows), :]


def fold_kernel(got_ref, keep_ref, send_ref):
    lead = (got_ref.shape[1] - keep_ref.shape[1]) // (lax.axis_size("month") - 1)
    got = got_ref[...]
    total = jnp.sum(got.reshape(got.shape[0] // 8, 8, got.shape[1]), axis=0)
    total = jnp.sum(total, axis=0, keepdims=True)
    zero, one, half = total[:, :lead], total[:, lead : 2 * lead], total[:, 2 * lead :]
    first = lax.axis_index("month") == 0
    keep_ref[...] = jnp.concatenate([jnp.where(first, zero, one), half], axis=1)
    send_ref[...] = jnp.concatenate([jnp.where(first, one, zero), half], axis=1)


def last_kernel(keep_ref, swapped_ref, gram_b_ref, out_ref):
    rank = gram_b_ref.shape[0]
    lead = out_ref.shape[0] * rank
    keep, swapped = keep_ref[...], swapped_ref[...]
    rows = keep[:, :lead] + swapped[:, :lead]
    own = jnp.concatenate([rows[:, j * rank : (j + 1) * rank] for j in range(out_ref.shape[0])], axis=0)
    end = lead + rank * rank // 4
    first = lax.axis_index("month") == 0
    block, triangles = jnp.where(first, keep, swapped), jnp.where(first, swapped, keep)
    gram = unpack_gram(block[:, lead:end], triangles[:, lead:end], triangles[:, end : end + rank // 2])
    square_row, square_col = diagonals(gram)
    scale_row = jnp.sqrt(square_row + epsilon)
    scale_col = jnp.sqrt(square_col + epsilon)
    system = gram / scale_col / scale_row * gram_b_ref[...]
    out_ref[...] = dot32(own / scale_row, spd_inverse(system), ((1,), (0,)))


def shards(tile_values, prov_block, month_block, factor_b, factor_c):
    tiles, tile_i, tile_j, tile_k = tile_values.shape
    rank = factor_b.shape[1]
    n_prov = lax.axis_size(PROV)
    n_month = lax.axis_size("month")
    n_bin = lax.axis_size(BIN)
    month = lax.axis_index("month")
    bin_at = lax.axis_index(BIN)

    n_all = n_prov * n_month * n_bin
    c_rows = factor_c.shape[0] // n_month
    b_rep = n_bin // factor_b.shape[0]
    parts = 8
    sent = pl.pallas_call(
        spread_kernel,
        out_shape=jax.ShapeDtypeStruct((n_all, 2, c_rows * rank), factor_c.dtype),
        in_specs=[pl.BlockSpec(memory_space=pltpu.VMEM)] * 2,
        out_specs=pl.BlockSpec(memory_space=pl.ANY),
        scratch_shapes=[
            pltpu.VMEM((n_all // parts, 2, c_rows * rank), factor_c.dtype),
            pltpu.SemaphoreType.DMA((parts,)),
        ],
        compiler_params=pltpu.CompilerParams(vmem_limit_bytes=60 * 1024 * 1024),
        name="spread_rows",
    )(factor_c, factor_b)
    got = lax.all_to_all(sent, PROV + BIN + ("month",), 0, 0, tiled=True)
    pairs_c = got[:, 0, :]
    twice_b = got[:, 1, :].reshape(n_prov, factor_b.shape[0], b_rep, n_month, c_rows * rank)[:, :, 0]
    twice_b = twice_b.transpose(0, 2, 1, 3).reshape(-1, c_rows * rank)

    slab_pairs = lax.dynamic_slice_in_dim(pairs_c, bin_at * (tile_k // c_rows), tile_k // c_rows, 0)
    slab_c = slab_pairs.reshape(tile_k, rank)
    slab_b = lax.dynamic_slice_in_dim(twice_b, month * (MB_DEV * tile_j), MB_DEV * tile_j, 0)
    slab_b = slab_b.astype(jnp.float32).reshape(MB_DEV, tile_j, c_rows * rank)

    smem, vmem, hbm = (pl.BlockSpec(memory_space=space) for space in (pltpu.SMEM, pltpu.VMEM, pl.ANY))
    kept = pl.pallas_call(
        keep_kernel,
        out_shape=jax.ShapeDtypeStruct((KEPT,) + tile_values.shape[1:], tile_values.dtype),
        in_specs=[hbm],
        out_specs=vmem,
        scratch_shapes=[pltpu.SemaphoreType.DMA],
        compiler_params=LARGE,
        name="keep_tiles",
    )(tile_values)
    late = tiles - KEPT
    tile_scratch = [
        pltpu.VMEM((late,) + tile_values.shape[1:], tile_values.dtype),
        pltpu.SemaphoreType.DMA((late,)),
    ]
    half = tile_i // 2
    prov_at = jnp.clip(prov_block, 0, PB_DEV - 1)
    month_at = jnp.clip(jnp.concatenate([month_block, month[None]]), 0, MB_DEV - 1)
    swap = [(i, n_month - 1 - i) for i in range(n_month)]
    block_at = prov_at ^ (month * n_bin)
    sums = jax.ShapeDtypeStruct((n_bin, half, 2 * rank), jnp.float32)
    own_half, other_half = pl.pallas_call(
        first_product_kernel,
        out_shape=(sums, sums),
        in_specs=[smem, smem, hbm, vmem, vmem, vmem],
        out_specs=(vmem, vmem),
        scratch_shapes=tile_scratch,
        compiler_params=LARGE,
        name="first_product",
    )(block_at, month_at, tile_values, kept, slab_c, slab_b)

    twice_b, pairs_c, own_half, other_half = lax.optimization_barrier((twice_b, pairs_c, own_half, other_half))
    arrived = lax.ppermute(other_half, "month", swap)
    square = jax.ShapeDtypeStruct((rank, rank), jnp.float32)
    inverse, gram_b = pl.pallas_call(
        first_inverse_kernel,
        out_shape=(square, square),
        cost_estimate=pl.CostEstimate(flops=20000000, bytes_accessed=200000, transcendentals=0),
        name="first_inverse",
        compiler_params=SMALL,
    )(twice_b, pairs_c)
    inverse, arrived = lax.optimization_barrier((inverse, arrived))
    own_a = lax.all_to_all(own_half + arrived, BIN, 0, 0, tiled=True)
    spread, factor_a = pl.pallas_call(
        solve_kernel,
        out_shape=(
            jax.ShapeDtypeStruct(own_a.shape, jnp.float32),
            jax.ShapeDtypeStruct((tile_i, rank), jnp.float32),
        ),
        compiler_params=SMALL,
        name="solve_first",
    )(own_a, inverse)

    half_a = lax.all_to_all(spread, BIN, 0, 0, tiled=True)
    other_a = lax.ppermute(half_a, "month", swap)

    n_out = n_prov * n_month
    out_rows = tile_k // n_out
    partial_c, packed = pl.pallas_call(
        last_product_kernel,
        out_shape=(
            jax.ShapeDtypeStruct((n_out, out_rows * rank), jnp.float32),
            jax.ShapeDtypeStruct((rank // 8 + 1, 2 * rank), jnp.float32),
        ),
        in_specs=[smem, smem, hbm, vmem, vmem, vmem, vmem],
        out_specs=(vmem, vmem),
        scratch_shapes=tile_scratch + [pltpu.VMEM((tile_k, rank), jnp.float32)],
        compiler_params=LARGE,
        name="last_product",
    )(block_at, month_at, tile_values, kept, half_a, other_a, slab_b)

    sent_gram = jnp.broadcast_to(packed.reshape(1, 1, -1), (n_prov, 1, packed.size))
    last = jnp.concatenate([partial_c.reshape(n_prov, 1, -1), sent_gram], axis=2)
    last = lax.all_to_all(last, PROV, 0, 0, tiled=True)
    summed = jax.ShapeDtypeStruct((1, out_rows * rank + packed.size), jnp.float32)
    keep, send = pl.pallas_call(
        fold_kernel, out_shape=(summed, summed), compiler_params=SMALL, name="fold_sources"
    )(last.reshape(n_prov, -1))
    new_c = pl.pallas_call(
        last_kernel,
        out_shape=jax.ShapeDtypeStruct((out_rows, rank), jnp.float32),
        compiler_params=SMALL,
        name="last_solve",
    )(keep, lax.ppermute(send, "month", swap), gram_b)
    return (factor_a, new_c)


def solution(mesh):
    prov, month, bins = mesh.devices.shape
    shape = (prov // 8, 8, month, bins // 2, 2)
    mesh = jax.sharding.Mesh(mesh.devices.reshape(shape), ("zl", "y", "month", "x", "zh"))
    everywhere = PROV + ("month",) + BIN
    in_specs = (
        P(everywhere, None, None, None),
        P(everywhere),
        P(everywhere),
        P(PROV + ("month",), None),
        P(PROV + BIN, None),
    )
    out_specs = (P(everywhere, None), P(BIN + PROV + ("month",), None))
    return jax.shard_map(shards, mesh=mesh, in_specs=in_specs, out_specs=out_specs, check_vma=False)
```

```python
import jax
import jax.numpy as jnp
from jax import lax
from jax.experimental import pallas as pl
from jax.experimental.pallas import tpu as pltpu
from jax.sharding import PartitionSpec as P

MB_DEV = 8
KEPT = 5
PB_DEV = 16
epsilon = 1e-06
HIGH = lax.Precision.HIGHEST
SMALL = pltpu.CompilerParams(vmem_limit_bytes=8 * 1024 * 1024)
LARGE = pltpu.CompilerParams(vmem_limit_bytes=50 * 1024 * 1024)
PROV = ("zl", "y")
BIN = ("x", "zh")


def dot32(a, b, dims, precision=HIGH):
    return lax.dot_general(a, b, (dims, ((), ())), precision=precision, preferred_element_type=jnp.float32)


def diagonals(a):
    lane = lax.broadcasted_iota(jnp.int32, a.shape, 1)
    sub = lax.broadcasted_iota(jnp.int32, a.shape, 0)
    diag = jnp.where(lane == sub, a, 0.0)
    return jnp.sum(diag, axis=0, keepdims=True), jnp.sum(diag, axis=1, keepdims=True)


def spd_inverse(a):
    n = a.shape[0]
    in_row, in_col = diagonals(a)
    in_row, in_col = lax.rsqrt(in_row), lax.rsqrt(in_col)
    a = a * in_col * in_row
    lane = lax.broadcasted_iota(jnp.int32, a.shape, 1)
    sub = lax.broadcasted_iota(jnp.int32, a.shape, 0)
    lane_row = lax.broadcasted_iota(jnp.int32, (1, n), 1)
    for k in range(0, n, 4):
        cols = [jnp.broadcast_to(a[:, k + j : k + j + 1], a.shape) for j in range(4)]
        (p00, p01, p02, p03), (_, p11, p12, p13), (_, _, p22, p23), (_, _, _, p33) = [
            [cols[j][k + i : k + i + 1] for j in range(4)] for i in range(4)
        ]
        inv = 1.0 / (p00 * p11 - p01 * p01)
        e00, e01, e11 = p11 * inv, -p01 * inv, p00 * inv
        w00, w01 = e00 * p02 + e01 * p12, e00 * p03 + e01 * p13
        w10, w11 = e01 * p02 + e11 * p12, e01 * p03 + e11 * p13
        s00, s01 = p22 - (p02 * w00 + p12 * w10), p23 - (p02 * w01 + p12 * w11)
        s11 = p33 - (p03 * w01 + p13 * w11)
        inv = 1.0 / (s00 * s11 - s01 * s01)
        q22, q23, q33 = s11 * inv, -s01 * inv, s00 * inv
        v00, v01 = w00 * q22 + w01 * q23, w00 * q23 + w01 * q33
        v10, v11 = w10 * q22 + w11 * q23, w10 * q23 + w11 * q33
        q01 = e01 + v00 * w10 + v01 * w11
        pivot = (
            (e00 + v00 * w00 + v01 * w01, q01, -v00, -v01),
            (q01, e11 + v10 * w10 + v11 * w11, -v10, -v11),
            (-v00, -v10, q22, q23),
            (-v01, -v11, q23, q33),
        )
        rows = [a[k + j : k + j + 1] for j in range(4)]
        rest = jnp.where((lane >= k) & (lane < k + 4), 0.0, a)
        fresh = []
        for i in range(4):
            q = pivot[i]
            new = (q[0] * rows[0] + q[1] * rows[1]) + (q[2] * rows[2] + q[3] * rows[3])
            for j in range(4):
                new = jnp.where(lane_row == k + j, q[j], new)
            fresh.append(new)
        a = rest - ((cols[0] * fresh[0] + cols[1] * fresh[1]) + (cols[2] * fresh[2] + cols[3] * fresh[3]))
        for i in range(4):
            a = jnp.where(sub == k + i, fresh[i], a)
    return a * in_col * in_row


def first_inverse_kernel(b_ref, pairs_ref, inv_ref, gram_b_ref):
    rank = inv_ref.shape[0]
    b = b_ref[:, :rank]
    gram_b = dot32(b, b, ((0,), (0,)), None)
    z = pairs_ref[...]
    twin = dot32(z, z, ((0,), (0,)), None)
    gram_c = twin[:rank, :rank] + twin[rank:, rank:]
    gram_b_ref[...] = gram_b
    inv_ref[...] = spd_inverse(gram_b * gram_c)


def spread_kernel(c_ref, b_ref, out_ref, chunk, sems):
    month = lax.axis_index("month")
    bin_at = lax.axis_index("x") * lax.axis_size("zh") + lax.axis_index("zh")
    c, b = c_ref[...].astype(jnp.float32), b_ref[...].astype(jnp.float32)
    rows = lax.broadcasted_iota(jnp.int32, c.shape, 0)

    def row(values, at):
        return jnp.sum(jnp.where(rows == at, values, 0.0), axis=0, keepdims=True)

    c_rows = c.shape[0] // lax.axis_size("month")
    b_row = row(b, bin_at // (lax.axis_size(BIN) // b.shape[0]))
    first = jnp.concatenate([row(c, month * c_rows + k) for k in range(c_rows)], axis=1)
    both = jnp.concatenate([first] + [jnp.concatenate([b_row] * c_rows, axis=1)], axis=0)
    chunk[...] = jnp.broadcast_to(both.astype(chunk.dtype)[None], chunk.shape)
    size = chunk.shape[0]
    copies = [
        pltpu.make_async_copy(chunk, out_ref.at[pl.ds(k * size, size)], sems.at[k]) for k in range(out_ref.shape[0] // size)
    ]
    for copy in copies:
        copy.start()
    for copy in copies:
        copy.wait()


def keep_kernel(tiles_ref, kept_ref, sem):
    copy = pltpu.make_async_copy(tiles_ref.at[pl.ds(0, kept_ref.shape[0])], kept_ref, sem)
    copy.start()
    copy.wait()


def tile_copies(tiles_ref, late, sems):
    kept = tiles_ref.shape[0] - late.shape[0]
    copies = [pltpu.make_async_copy(tiles_ref.at[kept + t], late.at[t], sems.at[t]) for t in range(late.shape[0])]
    for copy in copies:
        copy.start()
    return [None] * kept + copies


def both_halves(kept_ref, late, t, start, size):
    kept, tile_i, tile_j, tile_k = kept_ref.shape
    tile, at = (kept_ref, t) if t < kept else (late, t - kept)
    upper = tile[at, start : start + size].reshape(size * tile_j, tile_k)
    lower = tile[at, tile_i // 2 + start : tile_i // 2 + start + size].reshape(size * tile_j, tile_k)
    return jnp.concatenate([upper, lower], axis=1)


def first_product_kernel(where_ref, tiles_ref, kept_ref, c_ref, b_ref, own_ref, other_ref, late, sems):
    copies = tile_copies(tiles_ref, late, sems)
    own_ref[...] = jnp.zeros_like(own_ref)
    other_ref[...] = jnp.zeros_like(other_ref)
    c = c_ref[...]
    blocks = own_ref.shape[0]
    zero = jnp.zeros_like(c)
    twice_c = jnp.concatenate([jnp.concatenate([c, zero], axis=1), jnp.concatenate([zero, c], axis=1)], axis=0)
    half, tile_j = tiles_ref.shape[1] // 2, tiles_ref.shape[2]
    size = half // 4
    for t, copy in enumerate(copies):
        if copy is not None:
            copy.wait()
        at = where_ref[t]
        b = b_ref[where_ref[tiles_ref.shape[0] + t]][None]
        for start in range(0, half, size):
            product = dot32(both_halves(kept_ref, late, t, start, size), twice_c, ((1,), (0,)), None)
            product = product.reshape(size, tile_j, -1) * b
            product = jnp.sum(product, axis=1)
            rows = pl.ds(start, size)
            own_ref[at % blocks, rows] += jnp.where(at < blocks, product, 0.0)
            other_ref[at % blocks, rows] += jnp.where(at < blocks, 0.0, product)


def solve_kernel(got_ref, inv_ref, out_ref, own_ref):
    rank = inv_ref.shape[0]
    total = got_ref[0]
    for source in range(1, got_ref.shape[0]):
        total = total + got_ref[source]
    inv = inv_ref[...]
    upper = dot32(total[:, :rank], inv, ((1,), (0,)))
    lower = dot32(total[:, rank:], inv, ((1,), (0,)))
    solved = jnp.concatenate([upper, lower], axis=1)
    for target in range(out_ref.shape[0]):
        out_ref[target] = solved
    own_ref[: upper.shape[0]] = upper
    own_ref[upper.shape[0] :] = lower


def iotas(n):
    return lax.broadcasted_iota(jnp.int32, (n, n), 0), lax.broadcasted_iota(jnp.int32, (n, n), 1)


def pack_gram(gram, month):
    n = gram.shape[0] // 2
    row, column = iotas(n)
    last = gram[n:, n:]
    triangles = jnp.where(row >= column, gram[:n, :n], last)
    mine = jnp.where(month == 0, gram[:n, n:], triangles)
    per = n // 4
    folded = jnp.concatenate([mine[k * per : (k + 1) * per] for k in range(4)], axis=1)
    diagonal = jnp.sum(jnp.where(row == column, last, 0.0), axis=0, keepdims=True)
    return folded, jnp.concatenate([diagonal, jnp.zeros((1, 3 * n), jnp.float32)], axis=1)


def unpack_gram(block, triangles, diagonal):
    n = diagonal.shape[1]
    row, column = iotas(n)

    def square(flat):
        rows = jnp.concatenate([flat[:, k * 4 * n : (k + 1) * 4 * n] for k in range(n // 4)], axis=0)
        return jnp.concatenate([rows[:, k * n : (k + 1) * n] for k in range(4)], axis=0)

    block, triangles = square(block), square(triangles)
    turned = triangles.T
    first = jnp.where(row >= column, triangles, turned)
    last = jnp.where(row < column, triangles, jnp.where(row > column, turned, diagonal))
    return jnp.concatenate(
        [jnp.concatenate([first, block], axis=1), jnp.concatenate([block.T, last], axis=1)], axis=0
    )


def last_product_kernel(where_ref, tiles_ref, kept_ref, a_ref, other_ref, b_ref, out_ref, gram_ref, late, sems, turned):
    copies = tile_copies(tiles_ref, late, sems)
    blocks, half, lanes = a_ref.shape
    rank, tile_j, tile_k = lanes // 2, tiles_ref.shape[2], tiles_ref.shape[3]
    size = half // 4
    own, other = (ref[...].reshape(blocks * half, lanes) for ref in (a_ref, other_ref))
    twin = dot32(own, own, ((0,), (0,))) + dot32(other, other, ((0,), (0,)))
    folded, diagonal = pack_gram(twin[:rank, :rank] + twin[rank:, rank:], lax.axis_index("month"))
    gram_ref[: folded.shape[0]] = folded
    gram_ref[folded.shape[0] :] = diagonal
    total = None
    for t, copy in enumerate(copies):
        if copy is not None:
            copy.wait()
        at = where_ref[t]
        b = b_ref[where_ref[tiles_ref.shape[0] + t]][None]
        for start in range(0, half, size):
            rows = pl.ds(start, size)
            a = jnp.where(at < blocks, a_ref[at % blocks, rows], other_ref[at % blocks, rows])
            joint = (a[:, None, :] * b).reshape(size * tile_j, lanes).T
            high = joint.astype(jnp.bfloat16)
            low = (joint - high.astype(jnp.float32)).astype(jnp.bfloat16)
            both = jnp.concatenate([high, low], axis=0)
            part = dot32(both, both_halves(kept_ref, late, t, start, size), ((1,), (0,)), None)
            total = part if total is None else total + part
    parts = [total[k * rank : (k + 1) * rank, (k % 2) * tile_k : (k % 2 + 1) * tile_k] for k in range(4)]
    turned[...] = (parts[0] + parts[1] + parts[2] + parts[3]).T
    out_rows = lanes // rank
    for row in range(out_rows):
        out_ref[:, row * rank : (row + 1) * rank] = turned[pl.ds(row, tile_k // out_rows, stride=out_rows), :]


def fold_kernel(got_ref, keep_ref, send_ref):
    lead = (got_ref.shape[1] - keep_ref.shape[1]) // (lax.axis_size("month") - 1)
    got = got_ref[...]
    total = jnp.sum(got.reshape(got.shape[0] // 8, 8, got.shape[1]), axis=0)
    total = jnp.sum(total, axis=0, keepdims=True)
    zero, one, half = total[:, :lead], total[:, lead : 2 * lead], total[:, 2 * lead :]
    first = lax.axis_index("month") == 0
    keep_ref[...] = jnp.concatenate([jnp.where(first, zero, one), half], axis=1)
    send_ref[...] = jnp.concatenate([jnp.where(first, one, zero), half], axis=1)


def last_kernel(keep_ref, swapped_ref, gram_b_ref, out_ref):
    rank = gram_b_ref.shape[0]
    lead = out_ref.shape[0] * rank
    keep, swapped = keep_ref[...], swapped_ref[...]
    rows = keep[:, :lead] + swapped[:, :lead]
    own = jnp.concatenate([rows[:, j * rank : (j + 1) * rank] for j in range(out_ref.shape[0])], axis=0)
    end = lead + rank * rank // 4
    first = lax.axis_index("month") == 0
    block, triangles = jnp.where(first, keep, swapped), jnp.where(first, swapped, keep)
    gram = unpack_gram(block[:, lead:end], triangles[:, lead:end], triangles[:, end : end + rank // 2])
    square_row, square_col = diagonals(gram)
    scale_row = jnp.sqrt(square_row + epsilon)
    scale_col = jnp.sqrt(square_col + epsilon)
    system = gram / scale_col / scale_row * gram_b_ref[...]
    out_ref[...] = dot32(own / scale_row, spd_inverse(system), ((1,), (0,)))


def shards(tile_values, prov_block, month_block, factor_b, factor_c):
    tiles, tile_i, tile_j, tile_k = tile_values.shape
    rank = factor_b.shape[1]
    n_prov = lax.axis_size(PROV)
    n_month = lax.axis_size("month")
    n_bin = lax.axis_size(BIN)
    month = lax.axis_index("month")
    bin_at = lax.axis_index(BIN)

    n_all = n_prov * n_month * n_bin
    c_rows = factor_c.shape[0] // n_month
    b_rep = n_bin // factor_b.shape[0]
    parts = 8
    sent = pl.pallas_call(
        spread_kernel,
        out_shape=jax.ShapeDtypeStruct((n_all, 2, c_rows * rank), factor_c.dtype),
        in_specs=[pl.BlockSpec(memory_space=pltpu.VMEM)] * 2,
        out_specs=pl.BlockSpec(memory_space=pl.ANY),
        scratch_shapes=[
            pltpu.VMEM((n_all // parts, 2, c_rows * rank), factor_c.dtype),
            pltpu.SemaphoreType.DMA((parts,)),
        ],
        compiler_params=pltpu.CompilerParams(vmem_limit_bytes=60 * 1024 * 1024),
        name="spread_rows",
    )(factor_c, factor_b)
    got = lax.all_to_all(sent, PROV + BIN + ("month",), 0, 0, tiled=True)
    pairs_c = got[:, 0, :]
    twice_b = got[:, 1, :].reshape(n_prov, factor_b.shape[0], b_rep, n_month, c_rows * rank)[:, :, 0]
    twice_b = twice_b.transpose(0, 2, 1, 3).reshape(-1, c_rows * rank)

    slab_pairs = lax.dynamic_slice_in_dim(pairs_c, bin_at * (tile_k // c_rows), tile_k // c_rows, 0)
    slab_c = slab_pairs.reshape(tile_k, rank)
    slab_b = lax.dynamic_slice_in_dim(twice_b, month * (MB_DEV * tile_j), MB_DEV * tile_j, 0)
    slab_b = slab_b.astype(jnp.float32).reshape(MB_DEV, tile_j, c_rows * rank)

    smem, vmem, hbm = (pl.BlockSpec(memory_space=space) for space in (pltpu.SMEM, pltpu.VMEM, pl.ANY))
    kept = pl.pallas_call(
        keep_kernel,
        out_shape=jax.ShapeDtypeStruct((KEPT,) + tile_values.shape[1:], tile_values.dtype),
        in_specs=[hbm],
        out_specs=vmem,
        scratch_shapes=[pltpu.SemaphoreType.DMA],
        compiler_params=LARGE,
        name="keep_tiles",
    )(tile_values)
    late = tiles - KEPT
    tile_scratch = [
        pltpu.VMEM((late,) + tile_values.shape[1:], tile_values.dtype),
        pltpu.SemaphoreType.DMA((late,)),
    ]
    half = tile_i // 2
    prov_at = jnp.clip(prov_block, 0, PB_DEV - 1)
    month_at = jnp.clip(month_block, 0, MB_DEV - 1)
    swap = [(i, n_month - 1 - i) for i in range(n_month)]
    where = jnp.concatenate([prov_at ^ (month * n_bin), month_at])
    sums = jax.ShapeDtypeStruct((n_bin, half, 2 * rank), jnp.float32)
    own_half, other_half = pl.pallas_call(
        first_product_kernel,
        out_shape=(sums, sums),
        in_specs=[smem, hbm, vmem, vmem, vmem],
        out_specs=(vmem, vmem),
        scratch_shapes=tile_scratch,
        compiler_params=LARGE,
        name="first_product",
    )(where, tile_values, kept, slab_c, slab_b)

    pair_a = own_half + lax.ppermute(other_half, "month", swap)
    twice_b, pairs_c, pair_a = lax.optimization_barrier((twice_b, pairs_c, pair_a))
    own_a = lax.all_to_all(pair_a, BIN, 0, 0, tiled=True)

    square = jax.ShapeDtypeStruct((rank, rank), jnp.float32)
    inverse, gram_b = pl.pallas_call(
        first_inverse_kernel,
        out_shape=(square, square),
        cost_estimate=pl.CostEstimate(flops=20000000, bytes_accessed=200000, transcendentals=0),
        name="first_inverse",
        compiler_params=SMALL,
    )(twice_b, pairs_c)
    spread, factor_a = pl.pallas_call(
        solve_kernel,
        out_shape=(
            jax.ShapeDtypeStruct(own_a.shape, jnp.float32),
            jax.ShapeDtypeStruct((tile_i, rank), jnp.float32),
        ),
        compiler_params=SMALL,
        name="solve_first",
    )(own_a, inverse)

    half_a = lax.all_to_all(spread, BIN, 0, 0, tiled=True)
    other_a = lax.ppermute(half_a, "month", swap)

    n_out = n_prov * n_month
    out_rows = tile_k // n_out
    partial_c, packed = pl.pallas_call(
        last_product_kernel,
        out_shape=(
            jax.ShapeDtypeStruct((n_out, out_rows * rank), jnp.float32),
            jax.ShapeDtypeStruct((rank // 8 + 1, 2 * rank), jnp.float32),
        ),
        in_specs=[smem, hbm, vmem, vmem, vmem, vmem],
        out_specs=(vmem, vmem),
        scratch_shapes=tile_scratch + [pltpu.VMEM((tile_k, rank), jnp.float32)],
        compiler_params=LARGE,
        name="last_product",
    )(where, tile_values, kept, half_a, other_a, slab_b)

    sent_gram = jnp.broadcast_to(packed.reshape(1, 1, -1), (n_prov, 1, packed.size))
    last = jnp.concatenate([partial_c.reshape(n_prov, 1, -1), sent_gram], axis=2)
    last = lax.all_to_all(last, PROV, 0, 0, tiled=True)
    summed = jax.ShapeDtypeStruct((1, out_rows * rank + packed.size), jnp.float32)
    keep, send = pl.pallas_call(
        fold_kernel, out_shape=(summed, summed), compiler_params=SMALL, name="fold_sources"
    )(last.reshape(n_prov, -1))
    new_c = pl.pallas_call(
        last_kernel,
        out_shape=jax.ShapeDtypeStruct((out_rows, rank), jnp.float32),
        compiler_params=SMALL,
        name="last_solve",
    )(keep, lax.ppermute(send, "month", swap), gram_b)
    return (factor_a, new_c)


def solution(mesh):
    prov, month, bins = mesh.devices.shape
    shape = (prov // 8, 8, month, bins // 2, 2)
    mesh = jax.sharding.Mesh(mesh.devices.reshape(shape), ("zl", "y", "month", "x", "zh"))
    everywhere = PROV + ("month",) + BIN
    in_specs = (
        P(everywhere, None, None, None),
        P(everywhere),
        P(everywhere),
        P(PROV + ("month",), None),
        P(PROV + BIN, None),
    )
    out_specs = (P(everywhere, None), P(BIN + PROV + ("month",), None))
    return jax.shard_map(shards, mesh=mesh, in_specs=in_specs, out_specs=out_specs, check_vma=False)
```

```python
import jax
import jax.numpy as jnp
from jax import lax
from jax.experimental import pallas as pl
from jax.experimental.pallas import tpu as pltpu
from jax.sharding import PartitionSpec as P

MB_DEV = 8
KEPT = 5
PB_DEV = 16
epsilon = 1e-06
HIGH = lax.Precision.HIGHEST
SMALL = pltpu.CompilerParams(vmem_limit_bytes=8 * 1024 * 1024)
LARGE = pltpu.CompilerParams(vmem_limit_bytes=50 * 1024 * 1024)
PROV = ("zl", "y")
BIN = ("x", "zh")


def dot32(a, b, dims, precision=HIGH):
    return lax.dot_general(a, b, (dims, ((), ())), precision=precision, preferred_element_type=jnp.float32)


def diagonals(a):
    lane = lax.broadcasted_iota(jnp.int32, a.shape, 1)
    sub = lax.broadcasted_iota(jnp.int32, a.shape, 0)
    diag = jnp.where(lane == sub, a, 0.0)
    return jnp.sum(diag, axis=0, keepdims=True), jnp.sum(diag, axis=1, keepdims=True)


def spd_inverse(a):
    n = a.shape[0]
    in_row, in_col = diagonals(a)
    in_row, in_col = lax.rsqrt(in_row), lax.rsqrt(in_col)
    a = a * in_col * in_row
    lane = lax.broadcasted_iota(jnp.int32, a.shape, 1)
    sub = lax.broadcasted_iota(jnp.int32, a.shape, 0)
    lane_row = lax.broadcasted_iota(jnp.int32, (1, n), 1)
    for k in range(0, n, 4):
        cols = [jnp.broadcast_to(a[:, k + j : k + j + 1], a.shape) for j in range(4)]
        (p00, p01, p02, p03), (_, p11, p12, p13), (_, _, p22, p23), (_, _, _, p33) = [
            [cols[j][k + i : k + i + 1] for j in range(4)] for i in range(4)
        ]
        inv = 1.0 / (p00 * p11 - p01 * p01)
        e00, e01, e11 = p11 * inv, -p01 * inv, p00 * inv
        w00, w01 = e00 * p02 + e01 * p12, e00 * p03 + e01 * p13
        w10, w11 = e01 * p02 + e11 * p12, e01 * p03 + e11 * p13
        s00, s01 = p22 - (p02 * w00 + p12 * w10), p23 - (p02 * w01 + p12 * w11)
        s11 = p33 - (p03 * w01 + p13 * w11)
        inv = 1.0 / (s00 * s11 - s01 * s01)
        q22, q23, q33 = s11 * inv, -s01 * inv, s00 * inv
        v00, v01 = w00 * q22 + w01 * q23, w00 * q23 + w01 * q33
        v10, v11 = w10 * q22 + w11 * q23, w10 * q23 + w11 * q33
        q01 = e01 + v00 * w10 + v01 * w11
        pivot = (
            (e00 + v00 * w00 + v01 * w01, q01, -v00, -v01),
            (q01, e11 + v10 * w10 + v11 * w11, -v10, -v11),
            (-v00, -v10, q22, q23),
            (-v01, -v11, q23, q33),
        )
        rows = [a[k + j : k + j + 1] for j in range(4)]
        rest = jnp.where((lane >= k) & (lane < k + 4), 0.0, a)
        fresh = []
        for i in range(4):
            q = pivot[i]
            new = (q[0] * rows[0] + q[1] * rows[1]) + (q[2] * rows[2] + q[3] * rows[3])
            for j in range(4):
                new = jnp.where(lane_row == k + j, q[j], new)
            fresh.append(new)
        a = rest - ((cols[0] * fresh[0] + cols[1] * fresh[1]) + (cols[2] * fresh[2] + cols[3] * fresh[3]))
        for i in range(4):
            a = jnp.where(sub == k + i, fresh[i], a)
    return a * in_col * in_row


def first_inverse_kernel(b_ref, pairs_ref, inv_ref, gram_b_ref):
    rank = inv_ref.shape[0]
    b = b_ref[:, :rank]
    gram_b = dot32(b, b, ((0,), (0,)), None)
    z = pairs_ref[...]
    twin = dot32(z, z, ((0,), (0,)), None)
    gram_c = twin[:rank, :rank] + twin[rank:, rank:]
    gram_b_ref[...] = gram_b
    inv_ref[...] = spd_inverse(gram_b * gram_c)


def spread_kernel(c_ref, b_ref, out_ref, chunk, sems):
    month = lax.axis_index("month")
    bin_at = lax.axis_index("x") * lax.axis_size("zh") + lax.axis_index("zh")
    c, b = c_ref[...].astype(jnp.float32), b_ref[...].astype(jnp.float32)
    rows = lax.broadcasted_iota(jnp.int32, c.shape, 0)

    def row(values, at):
        return jnp.sum(jnp.where(rows == at, values, 0.0), axis=0, keepdims=True)

    c_rows = c.shape[0] // lax.axis_size("month")
    b_row = row(b, bin_at // (lax.axis_size(BIN) // b.shape[0]))
    first = jnp.concatenate([row(c, month * c_rows + k) for k in range(c_rows)], axis=1)
    both = jnp.concatenate([first] + [jnp.concatenate([b_row] * c_rows, axis=1)], axis=0)
    chunk[...] = jnp.broadcast_to(both.astype(chunk.dtype)[None], chunk.shape)
    size = chunk.shape[0]
    copies = [
        pltpu.make_async_copy(chunk, out_ref.at[pl.ds(k * size, size)], sems.at[k]) for k in range(out_ref.shape[0] // size)
    ]
    for copy in copies:
        copy.start()
    for copy in copies:
        copy.wait()


def keep_kernel(tiles_ref, kept_ref, sem):
    copy = pltpu.make_async_copy(tiles_ref.at[pl.ds(0, kept_ref.shape[0])], kept_ref, sem)
    copy.start()
    copy.wait()


def tile_copies(tiles_ref, late, sems):
    kept = tiles_ref.shape[0] - late.shape[0]
    copies = [pltpu.make_async_copy(tiles_ref.at[kept + t], late.at[t], sems.at[t]) for t in range(late.shape[0])]
    for copy in copies:
        copy.start()
    return [None] * kept + copies


def both_halves(kept_ref, late, t, start, size):
    kept, tile_i, tile_j, tile_k = kept_ref.shape
    tile, at = (kept_ref, t) if t < kept else (late, t - kept)
    upper = tile[at, start : start + size].reshape(size * tile_j, tile_k)
    lower = tile[at, tile_i // 2 + start : tile_i // 2 + start + size].reshape(size * tile_j, tile_k)
    return jnp.concatenate([upper, lower], axis=1)


def first_product_kernel(where_ref, tiles_ref, kept_ref, c_ref, b_ref, own_ref, other_ref, late, sems):
    copies = tile_copies(tiles_ref, late, sems)
    own_ref[...] = jnp.zeros_like(own_ref)
    other_ref[...] = jnp.zeros_like(other_ref)
    c = c_ref[...]
    blocks = own_ref.shape[0]
    zero = jnp.zeros_like(c)
    twice_c = jnp.concatenate([jnp.concatenate([c, zero], axis=1), jnp.concatenate([zero, c], axis=1)], axis=0)
    half, tile_j = tiles_ref.shape[1] // 2, tiles_ref.shape[2]
    size = half // 4
    for t, copy in enumerate(copies):
        if copy is not None:
            copy.wait()
        at = where_ref[t]
        b = b_ref[where_ref[tiles_ref.shape[0] + t]].astype(jnp.float32)[None]
        for start in range(0, half, size):
            product = dot32(both_halves(kept_ref, late, t, start, size), twice_c, ((1,), (0,)), None)
            product = product.reshape(size, tile_j, -1) * b
            product = jnp.sum(product, axis=1)
            rows = pl.ds(start, size)
            own_ref[at % blocks, rows] += jnp.where(at < blocks, product, 0.0)
            other_ref[at % blocks, rows] += jnp.where(at < blocks, 0.0, product)


def solve_kernel(got_ref, inv_ref, out_ref, own_ref):
    rank = inv_ref.shape[0]
    total = got_ref[0]
    for source in range(1, got_ref.shape[0]):
        total = total + got_ref[source]
    inv = inv_ref[...]
    upper = dot32(total[:, :rank], inv, ((1,), (0,)))
    lower = dot32(total[:, rank:], inv, ((1,), (0,)))
    solved = jnp.concatenate([upper, lower], axis=1)
    for target in range(out_ref.shape[0]):
        out_ref[target] = solved
    own_ref[: upper.shape[0]] = upper
    own_ref[upper.shape[0] :] = lower


def iotas(n):
    return lax.broadcasted_iota(jnp.int32, (n, n), 0), lax.broadcasted_iota(jnp.int32, (n, n), 1)


def pack_gram(gram, month):
    n = gram.shape[0] // 2
    row, column = iotas(n)
    last = gram[n:, n:]
    triangles = jnp.where(row >= column, gram[:n, :n], last)
    mine = jnp.where(month == 0, gram[:n, n:], triangles)
    per = n // 4
    folded = jnp.concatenate([mine[k * per : (k + 1) * per] for k in range(4)], axis=1)
    diagonal = jnp.sum(jnp.where(row == column, last, 0.0), axis=0, keepdims=True)
    return folded, jnp.concatenate([diagonal, jnp.zeros((1, 3 * n), jnp.float32)], axis=1)


def unpack_gram(block, triangles, diagonal):
    n = diagonal.shape[1]
    row, column = iotas(n)

    def square(flat):
        rows = jnp.concatenate([flat[:, k * 4 * n : (k + 1) * 4 * n] for k in range(n // 4)], axis=0)
        return jnp.concatenate([rows[:, k * n : (k + 1) * n] for k in range(4)], axis=0)

    block, triangles = square(block), square(triangles)
    turned = triangles.T
    first = jnp.where(row >= column, triangles, turned)
    last = jnp.where(row < column, triangles, jnp.where(row > column, turned, diagonal))
    return jnp.concatenate(
        [jnp.concatenate([first, block], axis=1), jnp.concatenate([block.T, last], axis=1)], axis=0
    )


def last_product_kernel(where_ref, tiles_ref, kept_ref, a_ref, other_ref, b_ref, out_ref, gram_ref, late, sems, turned):
    copies = tile_copies(tiles_ref, late, sems)
    blocks, half, lanes = a_ref.shape
    rank, tile_j, tile_k = lanes // 2, tiles_ref.shape[2], tiles_ref.shape[3]
    size = half // 4
    own, other = (ref[...].reshape(blocks * half, lanes) for ref in (a_ref, other_ref))
    twin = dot32(own, own, ((0,), (0,))) + dot32(other, other, ((0,), (0,)))
    folded, diagonal = pack_gram(twin[:rank, :rank] + twin[rank:, rank:], lax.axis_index("month"))
    gram_ref[: folded.shape[0]] = folded
    gram_ref[folded.shape[0] :] = diagonal
    total = None
    for t, copy in enumerate(copies):
        if copy is not None:
            copy.wait()
        at = where_ref[t]
        b = b_ref[where_ref[tiles_ref.shape[0] + t]].astype(jnp.float32)[None]
        for start in range(0, half, size):
            rows = pl.ds(start, size)
            a = jnp.where(at < blocks, a_ref[at % blocks, rows], other_ref[at % blocks, rows])
            joint = (a[:, None, :] * b).reshape(size * tile_j, lanes).T
            high = joint.astype(jnp.bfloat16)
            low = (joint - high.astype(jnp.float32)).astype(jnp.bfloat16)
            both = jnp.concatenate([high, low], axis=0)
            part = dot32(both, both_halves(kept_ref, late, t, start, size), ((1,), (0,)), None)
            total = part if total is None else total + part
    parts = [total[k * rank : (k + 1) * rank, (k % 2) * tile_k : (k % 2 + 1) * tile_k] for k in range(4)]
    turned[...] = (parts[0] + parts[1] + parts[2] + parts[3]).T
    out_rows = lanes // rank
    for row in range(out_rows):
        out_ref[:, row * rank : (row + 1) * rank] = turned[pl.ds(row, tile_k // out_rows, stride=out_rows), :]


def fold_kernel(got_ref, keep_ref, send_ref):
    lead = (got_ref.shape[1] - keep_ref.shape[1]) // (lax.axis_size("month") - 1)
    got = got_ref[...]
    total = jnp.sum(got.reshape(got.shape[0] // 8, 8, got.shape[1]), axis=0)
    total = jnp.sum(total, axis=0, keepdims=True)
    zero, one, half = total[:, :lead], total[:, lead : 2 * lead], total[:, 2 * lead :]
    first = lax.axis_index("month") == 0
    keep_ref[...] = jnp.concatenate([jnp.where(first, zero, one), half], axis=1)
    send_ref[...] = jnp.concatenate([jnp.where(first, one, zero), half], axis=1)


def last_kernel(keep_ref, swapped_ref, gram_b_ref, out_ref):
    rank = gram_b_ref.shape[0]
    lead = out_ref.shape[0] * rank
    keep, swapped = keep_ref[...], swapped_ref[...]
    rows = keep[:, :lead] + swapped[:, :lead]
    own = jnp.concatenate([rows[:, j * rank : (j + 1) * rank] for j in range(out_ref.shape[0])], axis=0)
    end = lead + rank * rank // 4
    first = lax.axis_index("month") == 0
    block, triangles = jnp.where(first, keep, swapped), jnp.where(first, swapped, keep)
    gram = unpack_gram(block[:, lead:end], triangles[:, lead:end], triangles[:, end : end + rank // 2])
    square_row, square_col = diagonals(gram)
    scale_row = jnp.sqrt(square_row + epsilon)
    scale_col = jnp.sqrt(square_col + epsilon)
    system = gram / scale_col / scale_row * gram_b_ref[...]
    out_ref[...] = dot32(own / scale_row, spd_inverse(system), ((1,), (0,)))


def shards(tile_values, prov_block, month_block, factor_b, factor_c):
    tiles, tile_i, tile_j, tile_k = tile_values.shape
    rank = factor_b.shape[1]
    n_prov = lax.axis_size(PROV)
    n_month = lax.axis_size("month")
    n_bin = lax.axis_size(BIN)
    month = lax.axis_index("month")
    bin_at = lax.axis_index(BIN)

    n_all = n_prov * n_month * n_bin
    c_rows = factor_c.shape[0] // n_month
    b_rep = n_bin // factor_b.shape[0]
    parts = 8
    sent = pl.pallas_call(
        spread_kernel,
        out_shape=jax.ShapeDtypeStruct((n_all, 2, c_rows * rank), factor_c.dtype),
        in_specs=[pl.BlockSpec(memory_space=pltpu.VMEM)] * 2,
        out_specs=pl.BlockSpec(memory_space=pl.ANY),
        scratch_shapes=[
            pltpu.VMEM((n_all // parts, 2, c_rows * rank), factor_c.dtype),
            pltpu.SemaphoreType.DMA((parts,)),
        ],
        compiler_params=pltpu.CompilerParams(vmem_limit_bytes=60 * 1024 * 1024),
        name="spread_rows",
    )(factor_c, factor_b)
    got = lax.all_to_all(sent, PROV + BIN + ("month",), 0, 0, tiled=True)
    pairs_c = got[:, 0, :]
    twice_b = got[:, 1, :].reshape(n_prov, factor_b.shape[0], b_rep, n_month, c_rows * rank)[:, :, 0]
    twice_b = twice_b.transpose(0, 2, 1, 3).reshape(-1, c_rows * rank)

    slab_pairs = lax.dynamic_slice_in_dim(pairs_c, bin_at * (tile_k // c_rows), tile_k // c_rows, 0)
    slab_c = slab_pairs.reshape(tile_k, rank)
    slab_b = lax.dynamic_slice_in_dim(twice_b, month * (MB_DEV * tile_j), MB_DEV * tile_j, 0)
    slab_b = slab_b.reshape(MB_DEV, tile_j, c_rows * rank)

    smem, vmem, hbm = (pl.BlockSpec(memory_space=space) for space in (pltpu.SMEM, pltpu.VMEM, pl.ANY))
    kept = pl.pallas_call(
        keep_kernel,
        out_shape=jax.ShapeDtypeStruct((KEPT,) + tile_values.shape[1:], tile_values.dtype),
        in_specs=[hbm],
        out_specs=vmem,
        scratch_shapes=[pltpu.SemaphoreType.DMA],
        compiler_params=LARGE,
        name="keep_tiles",
    )(tile_values)
    late = tiles - KEPT
    tile_scratch = [
        pltpu.VMEM((late,) + tile_values.shape[1:], tile_values.dtype),
        pltpu.SemaphoreType.DMA((late,)),
    ]
    half = tile_i // 2
    prov_at = jnp.clip(prov_block, 0, PB_DEV - 1)
    month_at = jnp.clip(month_block, 0, MB_DEV - 1)
    swap = [(i, n_month - 1 - i) for i in range(n_month)]
    where = jnp.concatenate([prov_at ^ (month * n_bin), month_at])
    sums = jax.ShapeDtypeStruct((n_bin, half, 2 * rank), jnp.float32)
    own_half, other_half = pl.pallas_call(
        first_product_kernel,
        out_shape=(sums, sums),
        in_specs=[smem, hbm, vmem, vmem, vmem],
        out_specs=(vmem, vmem),
        scratch_shapes=tile_scratch,
        compiler_params=LARGE,
        name="first_product",
    )(where, tile_values, kept, slab_c, slab_b)

    pair_a = own_half + lax.ppermute(other_half, "month", swap)
    twice_b, pairs_c, pair_a = lax.optimization_barrier((twice_b, pairs_c, pair_a))
    own_a = lax.all_to_all(pair_a, BIN, 0, 0, tiled=True)

    square = jax.ShapeDtypeStruct((rank, rank), jnp.float32)
    inverse, gram_b = pl.pallas_call(
        first_inverse_kernel,
        out_shape=(square, square),
        cost_estimate=pl.CostEstimate(flops=20000000, bytes_accessed=200000, transcendentals=0),
        name="first_inverse",
        compiler_params=SMALL,
    )(twice_b, pairs_c)
    spread, factor_a = pl.pallas_call(
        solve_kernel,
        out_shape=(
            jax.ShapeDtypeStruct(own_a.shape, jnp.float32),
            jax.ShapeDtypeStruct((tile_i, rank), jnp.float32),
        ),
        compiler_params=SMALL,
        name="solve_first",
    )(own_a, inverse)

    half_a = lax.all_to_all(spread, BIN, 0, 0, tiled=True)
    other_a = lax.ppermute(half_a, "month", swap)

    n_out = n_prov * n_month
    out_rows = tile_k // n_out
    partial_c, packed = pl.pallas_call(
        last_product_kernel,
        out_shape=(
            jax.ShapeDtypeStruct((n_out, out_rows * rank), jnp.float32),
            jax.ShapeDtypeStruct((rank // 8 + 1, 2 * rank), jnp.float32),
        ),
        in_specs=[smem, hbm, vmem, vmem, vmem, vmem],
        out_specs=(vmem, vmem),
        scratch_shapes=tile_scratch + [pltpu.VMEM((tile_k, rank), jnp.float32)],
        compiler_params=LARGE,
        name="last_product",
    )(where, tile_values, kept, half_a, other_a, slab_b)

    sent_gram = jnp.broadcast_to(packed.reshape(1, 1, -1), (n_prov, 1, packed.size))
    last = jnp.concatenate([partial_c.reshape(n_prov, 1, -1), sent_gram], axis=2)
    last = lax.all_to_all(last, PROV, 0, 0, tiled=True)
    summed = jax.ShapeDtypeStruct((1, out_rows * rank + packed.size), jnp.float32)
    keep, send = pl.pallas_call(
        fold_kernel, out_shape=(summed, summed), compiler_params=SMALL, name="fold_sources"
    )(last.reshape(n_prov, -1))
    new_c = pl.pallas_call(
        last_kernel,
        out_shape=jax.ShapeDtypeStruct((out_rows, rank), jnp.float32),
        compiler_params=SMALL,
        name="last_solve",
    )(keep, lax.ppermute(send, "month", swap), gram_b)
    return (factor_a, new_c)


def solution(mesh):
    prov, month, bins = mesh.devices.shape
    shape = (prov // 8, 8, month, bins // 2, 2)
    mesh = jax.sharding.Mesh(mesh.devices.reshape(shape), ("zl", "y", "month", "x", "zh"))
    everywhere = PROV + ("month",) + BIN
    in_specs = (
        P(everywhere, None, None, None),
        P(everywhere),
        P(everywhere),
        P(PROV + ("month",), None),
        P(PROV + BIN, None),
    )
    out_specs = (P(everywhere, None), P(BIN + PROV + ("month",), None))
    return jax.shard_map(shards, mesh=mesh, in_specs=in_specs, out_specs=out_specs, check_vma=False)
```
